32 devices in a mesh: leaf: 8 (over z, x), sub: 4 (over y, core).
Axes of the slice: x: 2, y: 2, z: 4, core: 2. Of those that a mesh axis runs over, the one named last changes fastest.
Arguments:
- coords: bfloat16 [4096, 3, 128], P('leaf'), may hold values from 0 to 4
- charges: bfloat16 [4096, 8, 128], P(('leaf', 'sub')), may hold values from -6 to 6
- counts: int32 [4096], P('leaf'), may hold values from 32 to 128, as said below
- morton: int32 [4096], P('leaf'), may hold values from 0 to 511, as said below
- near_list: int32 [4096, 27], P(('leaf', 'sub')), may hold values from -1 to 4095, as said below
- basis: bfloat16 [4096, 64, 128], P(('leaf', 'sub')), may hold values from -0.5 to 0.5
- transfer1: bfloat16 [4096, 64, 64], P(('leaf', 'sub')), may hold values from -0.75 to 0.75
- far2_list: int32 [512, 16], P(('leaf', 'sub')), may hold values from -1 to 511, as said below
- coupling2: bfloat16 [512, 16, 64, 64], P(('leaf', 'sub')), may hold values from -0.0625 to 0.0625
- transfer2: bfloat16 [512, 64, 64], P('leaf'), may hold values from -0.75 to 0.75
- far3_list: int32 [8, 8], P('leaf'), may hold values from -1 to 7, as said below
- coupling3: bfloat16 [8, 8, 64, 64], P('leaf'), may hold values from -0.01171875 to 0.01171875
Outputs:
- potential: float32 [4096, 8, 128], P(('leaf', 'sub'))
The draws below stay inside these ranges and needn't reach their ends.
Inputs may be any that keep to these rules, and one draw needn't show every extreme that they name: `counts`: each leaf's number of live points; leaves do not all have the same number. `morton`: within every block of 512 consecutive entries, a permutation of 0 to 511. `near_list`: row t starts with t itself; its other live entries are leaves other than t in the leaf group of t or in the group just before or after it; live entries come first and -1 fills the rest, with at least 13 live entries a row; entries may repeat. `far2_list`: row b names boxes other than b in the leaf group of b or in the group just before or after it; live entries come first and -1 fills the rest, with at least 8 live entries a row; entries may repeat. `far3_list`: row q names group boxes other than q; live entries come first and -1 fills the rest, with at least 4 live entries a row; entries may repeat.
All inputs are finite; a program needn't handle non-finite values.
Results may differ from the reference program's by a relative error of at most 0.011.
Values may be sent and summed in bfloat16 or wider, within the bound.
A program may use at most 64 MiB of HBM per device.

```python
import jax
import jax.numpy as jnp
from jax import lax

PTS = 128
RANK = 64
RHS = 8
NEAR = 27
FAR2 = 16
FAR3 = 8
GROUP = 512
LEAVES = 4096
BOXES2 = 512
BOXES3 = 8


def window_list(key, items, per_group, slots, keep_self, forced_item):
    index = jnp.arange(items, dtype=jnp.int32)
    owner = index // per_group
    groups = items // per_group
    lower = jnp.maximum(owner - 1, 0) * per_group
    upper = jnp.minimum(owner + 2, groups) * per_group
    pick_key, count_key = jax.random.split(key)
    raw = jax.random.randint(pick_key, (items, slots), 0, 1 << 20).astype(jnp.int32)
    picked = lower[:, None] + raw % (upper - lower - 1)[:, None]
    picked = jnp.where(picked >= index[:, None], picked + 1, picked)
    if keep_self:
        picked = picked.at[:, 0].set(index)
    else:
        picked = picked.at[forced_item, 0].set(items - 1)
    least = slots // 2
    live = least + jax.random.randint(count_key, (items,), 0, slots - least + 1).astype(jnp.int32)
    live = live.at[0].set(least)
    slot = jnp.arange(slots, dtype=jnp.int32)
    return jnp.where(slot[None, :] < live[:, None], picked, -1).astype(jnp.int32)


def draw_counts(key, part):
    values = jax.random.randint(key, (LEAVES,), PTS // 4, PTS + 1).astype(jnp.int32)
    return values.at[0].set(PTS).at[1].set(PTS // 4)


def group_order(key):
    return jax.random.permutation(key, GROUP).astype(jnp.int32)


def draw_morton(key, part):
    keys = jax.random.split(key, LEAVES // GROUP)
    return jax.vmap(group_order)(keys).reshape(LEAVES).astype(jnp.int32)


def draw_near_list(key, part):
    return window_list(key, LEAVES, GROUP, NEAR, True, 0)


def draw_far2_list(key, part):
    return window_list(key, BOXES2, BOXES2 // BOXES3, FAR2, False, BOXES2 - 2)


def draw_far3_list(key, part):
    return window_list(key, BOXES3, BOXES3, FAR3, False, 0)


def block_levels(own_key, shape, cuts, smallest, top_value):
    def one(axis_at, blocks):
        draws = jax.random.uniform(jax.random.fold_in(jax.random.fold_in(own_key, 6), axis_at), (blocks,), jnp.float32, smallest / len(cuts), top_value / len(cuts))
        return jnp.repeat(jnp.exp(draws), shape[axis_at] // blocks).reshape((-1,) + (1,) * (len(shape) - axis_at - 1))

    gain = one(*cuts[0])
    for cut in cuts[1:]:
        gain = gain * one(*cut)
    return gain


def gaussian(stream_key, extent, scale, most, cuts=(), kind=jnp.bfloat16):
    array = scale * jax.random.normal(stream_key, extent, jnp.float32)
    if cuts:
        array = array * block_levels(stream_key, extent, cuts, -0.22, 0.18)
    return jnp.clip(array, -most, most).astype(kind)


def setup_inputs(seed: int = 0) -> dict:
    streams_of = jax.random.split(jax.random.key(seed), 13)
    coords = jnp.clip(4.0 * jax.random.uniform(streams_of[0], (LEAVES, 3, PTS), jnp.float32) ** block_levels(streams_of[0], (LEAVES, 3, PTS), ((0, 8),), -0.2, 0.2), 0.0, 4.0).astype(jnp.bfloat16)
    charges = gaussian(streams_of[1], (LEAVES, RHS, PTS), 1.0, 6.0, ((0, 32),))
    counts = draw_counts(jax.random.fold_in(streams_of[12], 71), 0)
    morton = draw_morton(jax.random.fold_in(streams_of[12], 71), 0)
    near_list = draw_near_list(jax.random.fold_in(streams_of[12], 71), 0)
    basis = gaussian(streams_of[5], (LEAVES, RANK, PTS), PTS ** -0.5, 0.5, ((0, 32),))
    transfer1 = gaussian(streams_of[6], (LEAVES, RANK, RANK), RANK ** -0.5, 0.75, ((0, 32),))
    far2_list = draw_far2_list(jax.random.fold_in(streams_of[12], 71), 0)
    coupling2 = gaussian(streams_of[8], (BOXES2, FAR2, RANK, RANK), (RANK * FAR2 * 8) ** -0.5, 0.0625, ((0, 32),))
    transfer2 = gaussian(streams_of[9], (BOXES2, RANK, RANK), RANK ** -0.5, 0.75, ((0, 8),))
    far3_list = draw_far3_list(jax.random.fold_in(streams_of[12], 71), 0)
    coupling3 = gaussian(streams_of[11], (BOXES3, FAR3, RANK, RANK), (RANK * FAR3 * GROUP) ** -0.5, 0.01171875, ((0, 8),))
    return {"coords": coords, "charges": charges, "counts": counts, "morton": morton, "near_list": near_list, "basis": basis, "transfer1": transfer1, "far2_list": far2_list, "coupling2": coupling2, "transfer2": transfer2, "far3_list": far3_list, "coupling3": coupling3}


kernel_scale = 0.07957747154594767
delta_squared = 0.0025

def kernel_tile(targets, sources):
    squared = jnp.zeros((targets.shape[0], targets.shape[2], sources.shape[2]), jnp.float32)
    for component in range(3):
        offset = targets[:, component, :, None] - sources[:, component, None, :]
        squared = squared + offset * offset
    return (kernel_scale / jnp.sqrt(squared + delta_squared)).astype(jnp.bfloat16)

def far_field(moments, lists, couplings):
    valid = lists >= 0
    source = moments[jnp.maximum(lists, 0)].astype(jnp.float32)
    source = jnp.where(valid[..., None, None], source, jnp.zeros_like(source))
    return jnp.einsum('bkrc,bkcp->brp', source, couplings.astype(jnp.float32))

def reference(coords, charges, counts, morton, near_list, basis, transfer1, far2_list, coupling2, transfer2, far3_list, coupling3):
    leaf_ids = jnp.arange(LEAVES, dtype=jnp.int32)
    target_slot = leaf_ids // GROUP * GROUP + morton
    ordered = jnp.zeros_like(charges).at[target_slot].set(charges)
    live = jnp.arange(PTS, dtype=jnp.int32)[None, :] < counts[:, None]
    masked = jnp.where(live[:, None, :], ordered, jnp.zeros_like(ordered))
    leaf_moments = jnp.einsum('trp,tkp->trk', masked.astype(jnp.float32), basis.astype(jnp.float32)).astype(jnp.bfloat16)
    child_terms = jnp.einsum('trc,tcp->trp', leaf_moments.astype(jnp.float32), transfer1.astype(jnp.float32))
    box_moments = child_terms.reshape(BOXES2, 8, RHS, RANK).sum(axis=1).astype(jnp.bfloat16)
    box_terms = jnp.einsum('brc,bcp->brp', box_moments.astype(jnp.float32), transfer2.astype(jnp.float32))
    group_moments = box_terms.reshape(BOXES3, BOXES2 // BOXES3, RHS, RANK).sum(axis=1).astype(jnp.bfloat16)
    top_field = far_field(group_moments, far3_list, coupling3).astype(jnp.bfloat16)
    box_far = far_field(box_moments, far2_list, coupling2)
    parent_field = jnp.repeat(top_field, BOXES2 // BOXES3, axis=0).astype(jnp.float32)
    box_local = (box_far + jnp.einsum('brp,bcp->brc', parent_field, transfer2.astype(jnp.float32))).astype(jnp.bfloat16)
    spread = jnp.repeat(box_local, 8, axis=0).astype(jnp.float32)
    leaf_local = jnp.einsum('trp,tcp->trc', spread, transfer1.astype(jnp.float32)).astype(jnp.bfloat16)
    far_part = jnp.einsum('trk,tkp->trp', leaf_local.astype(jnp.float32), basis.astype(jnp.float32))
    coords_float = coords.astype(jnp.float32)

    def near_group(group):
        start = (group * GROUP).astype(jnp.int32)
        targets = lax.dynamic_slice_in_dim(coords_float, start, GROUP, 0)
        lists = lax.dynamic_slice_in_dim(near_list, start, GROUP, 0)

        def slot_step(total, column):
            valid = column >= 0
            index = jnp.maximum(column, 0)
            tile = kernel_tile(targets, coords_float[index]).astype(jnp.float32)
            source = masked[index].astype(jnp.float32)
            source = jnp.where(valid[:, None, None], source, jnp.zeros_like(source))
            return (total + jnp.einsum('tij,trj->tri', tile, source), None)
        total, unused = lax.scan(slot_step, jnp.zeros((GROUP, RHS, PTS), jnp.float32), lists.T)
        return total
    near_part = lax.map(near_group, jnp.arange(BOXES3, dtype=jnp.int32)).reshape(LEAVES, RHS, PTS)
    summed = near_part + far_part
    return jnp.where(live[:, None, :], summed, jnp.zeros_like(summed))
```

```python
import functools

import jax
import jax.numpy as jnp
from jax import lax
from jax.experimental import pallas as pl
from jax.experimental.pallas import tpu as pltpu
from jax.sharding import PartitionSpec as P

kernel_scale = 0.07957747154594767
delta_squared = 0.0025
SLOTS = 4
ITEMS = 4
FEATURES = 16


def shift(cells, axis, step):
    count = lax.axis_size(axis)
    if step > 0:
        pairs = [(i, i + 1) for i in range(count - 1)]
    else:
        pairs = [(i + 1, i) for i in range(count - 1)]
    return lax.ppermute(cells, axis, pairs)


def pieces(value):
    high = lax.reduce_precision(value, 8, 7)
    rest = value - high
    middle = lax.reduce_precision(rest, 8, 7)
    return high, middle, rest - middle


def features(planes, target):
    x, y, z = (planes[i].astype(jnp.float32) for i in range(3))
    norm = x * x + y * y + z * z
    one = jnp.ones_like(x)
    if target:
        rows = [x, y, z, *pieces(norm + delta_squared), one, one, one]
    else:
        rows = [-2.0 * x, -2.0 * y, -2.0 * z, one, one, one, *pieces(norm)]
    place = lax.broadcasted_iota(jnp.int32, (1, FEATURES, 1), 1)
    total = jnp.zeros((x.shape[0], FEATURES, x.shape[1]), jnp.float32)
    for k, row in enumerate(rows):
        total = jnp.where(place == k, row[:, None, :], total)
    return total.astype(jnp.bfloat16)


def far_field(moments, lists, couplings, offset):
    valid = lists >= 0
    local = jnp.clip(lists - offset, 0, moments.shape[0] - 1)
    source = jnp.where(valid[..., None, None], moments[local], jnp.zeros((), moments.dtype))
    return jnp.einsum("bkrc,bkcp->brp", source, couplings, preferred_element_type=jnp.float32)


def near_kernel(
    sizes,
    item_leaf,
    item_start,
    steps,
    near,
    inverse,
    counts,
    target_ref,
    own_features,
    halo_features,
    own_charges,
    halo_charges,
    far_ref,
    out_ref,
    feature_table,
    charge_table,
    target_table,
    squared,
    sems,
):
    leaf_dev, group_size, subs = sizes
    copies = [
        pltpu.make_async_copy(
            own_features, feature_table.at[pl.ds(group_size, group_size)], sems.at[0]
        ),
        pltpu.make_async_copy(
            halo_features.at[0], feature_table.at[pl.ds(0, group_size)], sems.at[1]
        ),
        pltpu.make_async_copy(
            halo_features.at[1], feature_table.at[pl.ds(2 * group_size, group_size)], sems.at[2]
        ),
        pltpu.make_async_copy(
            own_charges, charge_table.at[pl.ds(group_size, group_size)], sems.at[3]
        ),
    ]
    for lane in range(subs):
        for side in range(2):
            copies.append(
                pltpu.make_async_copy(
                    halo_charges.at[lane, side, pl.ds(0, leaf_dev)],
                    charge_table.at[pl.ds(2 * side * group_size + lane * leaf_dev, leaf_dev)],
                    sems.at[4 + 2 * lane + side],
                )
            )
    for copy in copies:
        copy.start()

    @pl.loop(0, leaf_dev // 8)
    def _(block):
        for u in range(8):
            t = block * 8 + u
            turned = target_ref[t].astype(jnp.float32).T
            target_table[t] = turned.astype(jnp.bfloat16)

    out_ref[...] = jnp.zeros_like(out_ref)
    for copy in copies:
        copy.wait()
    dead = 3 * group_size
    feature_table[dead] = feature_table[group_size]
    charge_table[dead] = jnp.zeros(charge_table.shape[1:], charge_table.dtype)

    def distances(step):
        for u in range(ITEMS):
            item = step * ITEMS + u
            t = jnp.minimum(item_leaf[item], leaf_dev - 1)
            p = item_start[item]
            rows = [feature_table[near[p + k]] for k in range(SLOTS)]
            squared[u] = jnp.dot(
                target_table[t],
                jnp.concatenate(rows, axis=1),
                preferred_element_type=jnp.float32,
            ).astype(jnp.bfloat16)

    def products(step):
        for u in range(ITEMS):
            item = step * ITEMS + u
            t = jnp.minimum(item_leaf[item], leaf_dev - 1)
            p = item_start[item]
            rows = [charge_table[inverse[near[p + k]]] for k in range(SLOTS)]
            out_ref[t] += lax.dot_general(
                jnp.concatenate(rows, axis=1),
                lax.rsqrt(squared[u]),
                (((1,), (1,)), ((), ())),
                preferred_element_type=jnp.float32,
            )

    distances(0)

    @pl.loop(1, steps[0] + 1)
    def _(step):
        products(step - 1)
        distances(step)

    place = lax.broadcasted_iota(jnp.int32, out_ref.shape[1:], 1)

    @pl.loop(0, leaf_dev // 8)
    def _(block):
        for u in range(8):
            t = block * 8 + u
            total = out_ref[t] * kernel_scale + far_ref[t]
            out_ref[t] = jnp.where(place < counts[t], total, 0.0)


def near_field(targets, own, halo, own_charges, halo_charges, near, inverse, counts, far, subs):
    leaf_dev, slots = near.shape
    group_size = own.shape[0]
    points = own.shape[2]
    dead = 3 * group_size
    chunks = -(-slots // SLOTS)
    live = jnp.sum((near >= 0).astype(jnp.int32), axis=1)
    used = (live + SLOTS - 1) // SLOTS
    ends = jnp.cumsum(used)
    capacity = leaf_dev * chunks + 2 * ITEMS
    item = jnp.arange(capacity, dtype=jnp.int32)
    before = ends[None, :] <= item[:, None]
    leaf = jnp.sum(before.astype(jnp.int32), axis=1)
    first = jnp.max(jnp.where(before, ends[None, :], 0), axis=1)
    row = chunks * SLOTS
    start = jnp.where(leaf < leaf_dev, leaf * row + SLOTS * (item - first), leaf_dev * row)
    steps = ((ends[-1:] + ITEMS - 1) // ITEMS).astype(jnp.int32)
    padded = jnp.pad(
        jnp.where(near >= 0, near, dead), ((0, 1), (0, row - slots)), constant_values=dead
    ).reshape(-1)
    smem = pl.BlockSpec(memory_space=pltpu.SMEM)
    vmem = pl.BlockSpec(memory_space=pltpu.VMEM)
    hbm = pl.BlockSpec(memory_space=pl.ANY)
    rhs = own_charges.shape[1]
    return pl.pallas_call(
        functools.partial(near_kernel, (leaf_dev, group_size, subs)),
        out_shape=jax.ShapeDtypeStruct((leaf_dev, rhs, points), jnp.float32),
        in_specs=[smem] * 6 + [vmem, hbm, hbm, hbm, hbm, vmem],
        out_specs=vmem,
        scratch_shapes=[
            pltpu.VMEM((dead + 1, FEATURES, points), jnp.bfloat16),
            pltpu.VMEM((dead + 1, rhs, points), jnp.bfloat16),
            pltpu.VMEM((leaf_dev, points, FEATURES), jnp.bfloat16),
            pltpu.VMEM((ITEMS, points, SLOTS * points), jnp.bfloat16),
            pltpu.SemaphoreType.DMA((4 + 2 * subs,)),
        ],
        compiler_params=pltpu.CompilerParams(vmem_limit_bytes=48 * 1024 * 1024),
        name="near_field",
    )(
        leaf.astype(jnp.int32),
        start.astype(jnp.int32),
        steps,
        padded,
        inverse,
        counts,
        targets,
        own,
        halo,
        own_charges,
        halo_charges,
        far,
    )


def on_device(
    coords,
    charges,
    counts,
    morton,
    near_list,
    basis,
    transfer1,
    far2_list,
    coupling2,
    transfer2,
    far3_list,
    coupling3,
):
    lane = lax.axis_index("sub")
    group = lax.axis_index("leaf")
    subs = lax.axis_size("sub")
    leaf_dev, rhs_count, points = charges.shape
    rank_size = basis.shape[1]
    group_size = coords.shape[0]
    clusters = far2_list.shape[0]
    group_boxes = transfer2.shape[0]
    start = lane * leaf_dev

    slot = lax.dynamic_slice_in_dim(morton, start, leaf_dev, 0)
    arriving_counts = counts[slot]
    place = jnp.arange(points, dtype=jnp.int32)
    masked = jnp.where(
        place[None, None, :] < arriving_counts[:, None, None], charges, jnp.zeros((), charges.dtype)
    )
    arrived = lax.all_gather(masked, "sub", axis=0, tiled=True)
    planes = coords.transpose(1, 0, 2)
    own_planes = lax.dynamic_slice_in_dim(planes, start, leaf_dev, 1)
    bundle = jnp.concatenate([masked, own_planes.reshape(-1, rhs_count, points)], axis=0)
    sides = jnp.stack([shift(bundle, "leaf", 1), shift(bundle, "leaf", -1)])
    halo = lax.all_gather(sides, "sub", axis=0)

    inverse = (
        jnp.zeros((group_size,), jnp.int32).at[morton].set(jnp.arange(group_size, dtype=jnp.int32))
    )
    all_inverse = jnp.concatenate(
        [
            shift(inverse, "leaf", 1),
            inverse + group_size,
            shift(inverse, "leaf", -1) + 2 * group_size,
            jnp.full((1,), 3 * group_size, jnp.int32),
        ]
    )
    own_features = features(planes, False)
    targets = features(own_planes, True)
    halo_planes = halo[:, :, leaf_dev:].reshape(subs, 2, 3, leaf_dev, points)
    halo_planes = halo_planes.transpose(2, 1, 0, 3, 4).reshape(3, 2 * group_size, points)
    halo_features = features(halo_planes, False).reshape(2, group_size, FEATURES, points)

    own_charges = arrived[lax.dynamic_slice_in_dim(inverse, start, leaf_dev, 0)]
    transfer_boxed = transfer1.reshape(clusters, 8, rank_size, rank_size)
    leaf_moments = jnp.einsum(
        "trp,tkp->trk", own_charges, basis, preferred_element_type=jnp.float32
    ).astype(jnp.bfloat16)
    box_moments = jnp.einsum(
        "bnrc,bncp->brp",
        leaf_moments.reshape(clusters, 8, rhs_count, rank_size),
        transfer_boxed,
        preferred_element_type=jnp.float32,
    ).astype(jnp.bfloat16)
    group_moments = lax.all_gather(box_moments, "sub", axis=0, tiled=True)
    top_moment = jnp.einsum(
        "brc,bcp->rp", group_moments, transfer2, preferred_element_type=jnp.float32
    ).astype(jnp.bfloat16)
    all_top = lax.all_gather(top_moment[None], "leaf", axis=0, tiled=True)
    near_boxes = jnp.concatenate(
        [shift(group_moments, "leaf", 1), group_moments, shift(group_moments, "leaf", -1)], axis=0
    )
    top_field = far_field(all_top, far3_list, coupling3, 0).astype(jnp.bfloat16)
    box_far = far_field(near_boxes, far2_list, coupling2, (group - 1) * group_boxes)
    own_transfer = lax.dynamic_slice_in_dim(transfer2, lane * clusters, clusters, 0)
    box_local = (
        box_far
        + jnp.einsum("rp,bcp->brc", top_field[0], own_transfer, preferred_element_type=jnp.float32)
    ).astype(jnp.bfloat16)
    leaf_local = jnp.einsum(
        "brp,bncp->bnrc", box_local, transfer_boxed, preferred_element_type=jnp.float32
    ).astype(jnp.bfloat16)
    leaf_local = leaf_local.reshape(leaf_dev, rhs_count, rank_size)
    far_part = jnp.einsum("trk,tkp->trp", leaf_local, basis, preferred_element_type=jnp.float32)

    base = (group - 1) * group_size
    near = jnp.where(near_list >= 0, near_list - base, -1)
    own_counts = lax.dynamic_slice_in_dim(counts, start, leaf_dev, 0)
    return near_field(
        targets,
        own_features,
        halo_features,
        arrived,
        halo,
        near,
        all_inverse,
        own_counts,
        far_part,
        subs,
    )


def solution(mesh):
    return jax.shard_map(
        on_device,
        mesh=mesh,
        in_specs=(
            P("leaf", None, None),
            P(("leaf", "sub"), None, None),
            P("leaf"),
            P("leaf"),
            P(("leaf", "sub"), None),
            P(("leaf", "sub"), None, None),
            P(("leaf", "sub"), None, None),
            P(("leaf", "sub"), None),
            P(("leaf", "sub"), None, None, None),
            P("leaf", None, None),
            P("leaf", None),
            P("leaf", None, None, None),
        ),
        out_specs=P(("leaf", "sub"), None, None),
        check_vma=False,
    )
```

```python
import functools

import jax
import jax.numpy as jnp
from jax import lax
from jax.experimental import pallas as pl
from jax.experimental.pallas import tpu as pltpu
from jax.sharding import PartitionSpec as P

kernel_scale = 0.07957747154594767
delta_squared = 0.0025
SLOTS = 4
ITEMS = 4
FEATURES = 16


MESH = pl.DeviceIdType.MESH


def pieces(value):
    high = lax.reduce_precision(value, 8, 7)
    rest = value - high
    middle = lax.reduce_precision(rest, 8, 7)
    return high, middle, rest - middle


def features(planes, target):
    x, y, z = (planes[i].astype(jnp.float32) for i in range(3))
    norm = x * x + y * y + z * z
    one = jnp.ones_like(x)
    if target:
        rows = [x, y, z, *pieces(norm + delta_squared), one, one, one]
    else:
        rows = [-2.0 * x, -2.0 * y, -2.0 * z, one, one, one, *pieces(norm)]
    place = lax.broadcasted_iota(jnp.int32, (1, FEATURES, 1), 1)
    total = jnp.zeros((x.shape[0], FEATURES, x.shape[1]), jnp.float32)
    for k, row in enumerate(rows):
        total = jnp.where(place == k, row[:, None, :], total)
    return total.astype(jnp.bfloat16)


NT = (((1,), (1,)), ((), ()))


def flip(lane, bit):
    return lane + bit - 2 * bit * ((lane // bit) % 2)


def matmul(left, right):
    return jnp.dot(left, right, preferred_element_type=jnp.float32)


def tree_kernel(
    groups,
    subs,
    positions,
    far2,
    far3,
    bundle,
    inverse,
    basis,
    transfer1,
    coupling2,
    transfer2,
    coupling3,
    own_table,
    halo,
    halo_inverse,
    far_ref,
    boxes,
    tops,
    box_far,
    local_sems,
    own_sems,
    side_sems,
    inverse_sems,
    halo_sems,
    box_sems,
    top_sems,
):
    group = lax.axis_index("leaf")
    lane = lax.axis_index("sub")
    leaf_dev = basis.shape[0]
    clusters = transfer1.shape[0]
    slots2 = far2.shape[1]
    slots3 = far3.shape[1]
    rank = basis.shape[1]
    before = (group + groups - 1) % groups
    after = (group + 1) % groups
    around = [((lane + d) % subs) for d in range(1, subs)]

    barrier = pltpu.get_barrier_semaphore()
    peers = [(group, other) for other in around]
    peers += [(side, other) for side in (before, after) for other in around]
    peers += [((group + d) % groups, lane) for d in range(1, groups)]
    for peer in peers:
        pl.semaphore_signal(barrier, inc=1, device_id=peer, device_id_type=MESH)
    pl.semaphore_wait(barrier, len(peers))

    def send(source, target, sems, index, device):
        copy = pltpu.make_async_remote_copy(
            src_ref=source,
            dst_ref=target,
            send_sem=sems.at[0, index],
            recv_sem=sems.at[1, index],
            device_id=device,
            device_id_type=MESH,
        )
        copy.start()
        return copy

    started = []
    bits = []
    bit = subs // 2
    while bit:
        bits.append(bit)
        bit //= 2

    charges = bundle.at[pl.ds(0, leaf_dev)]
    keep = [
        pltpu.make_async_copy(charges, own_table.at[lane], local_sems.at[0]),
    ]
    for copy in keep:
        copy.start()
    first = send(charges, own_table.at[lane], own_sems, 0, (group, flip(lane, bits[0])))
    started.append(first)
    sides = [
        send(bundle, halo.at[0, lane], side_sems, 0, (after, lane)),
        send(bundle, halo.at[1, lane], side_sems, 1, (before, lane)),
        send(inverse, halo_inverse.at[0], inverse_sems, 0, (after, lane)),
        send(inverse, halo_inverse.at[1], inverse_sems, 1, (before, lane)),
    ]
    started += sides
    for copy in keep:
        copy.wait()
    first.wait_recv()
    held = [lane, flip(lane, bits[0])]
    count = 1
    for bit in bits[1:]:
        copies = []
        for block in held:
            copies.append(
                send(
                    own_table.at[block],
                    own_table.at[block],
                    own_sems,
                    count,
                    (group, flip(lane, bit)),
                )
            )
            count += 1
        started += copies
        for copy in copies:
            copy.wait_recv()
        held = held + [flip(block, bit) for block in held]

    mine = boxes.at[1, lane]

    @pl.loop(0, clusters)
    def _(b):
        moments = []
        for u in range(8):
            position = positions[b * 8 + u]
            source = own_table[position // leaf_dev, position % leaf_dev]
            moments.append(
                lax.dot_general(
                    source, basis[b * 8 + u], NT, preferred_element_type=jnp.float32
                ).astype(jnp.bfloat16)
            )
        boxes[1, lane, b] = matmul(jnp.concatenate(moments, axis=1), transfer1[b]).astype(
            jnp.bfloat16
        )

    copies = []
    for other in around:
        copies.append(send(mine, boxes.at[1, lane], box_sems, len(copies), (group, other)))
    for other in [lane] + around:
        copies.append(send(mine, boxes.at[0, lane], box_sems, len(copies), (after, other)))
        copies.append(send(mine, boxes.at[2, lane], box_sems, len(copies), (before, other)))
    started += copies
    box_copies = copies

    for copy in sides:
        copy.wait_recv()
    held = [lane]
    count = 0
    halo_copies = []

    def forward(bit, held, count):
        copies = []
        for block in held:
            for side in range(2):
                copies.append(
                    send(
                        halo.at[side, block],
                        halo.at[side, block],
                        halo_sems,
                        count,
                        (group, flip(lane, bit)),
                    )
                )
                count += 1
        return copies, held + [flip(block, bit) for block in held], count

    halo_copies, held, count = forward(bits[0], held, count)
    started += halo_copies

    for copy in box_copies:
        copy.wait_recv()

    def top_step(chunk, total):
        cells = [boxes[1, chunk * 8 // clusters, chunk * 8 % clusters + u] for u in range(8)]
        return total + matmul(jnp.concatenate(cells, axis=1), transfer2[chunk])

    top = lax.fori_loop(
        0, subs * clusters // 8, top_step, jnp.zeros((bundle.shape[1], rank), jnp.float32)
    )
    tops[group] = top.astype(jnp.bfloat16)
    top_copies = [
        send(tops.at[group], tops.at[group], top_sems, d - 1, ((group + d) % groups, lane))
        for d in range(1, groups)
    ]
    started += top_copies

    @pl.loop(0, clusters)
    def _(b):
        cells = []
        for k in range(slots2):
            name = far2[b, k]
            local = jnp.clip(name - (group - 1) * subs * clusters, 0, 3 * subs * clusters - 1)
            side = local // (subs * clusters)
            rest = local % (subs * clusters)
            cell = boxes[side, rest // clusters, rest % clusters]
            cells.append(jnp.where(name >= 0, cell, jnp.zeros_like(cell)))
        box_far[b] = matmul(jnp.concatenate(cells, axis=1), coupling2[b])

    for bit in bits[1:]:
        for copy in halo_copies:
            copy.wait_recv()
        halo_copies, held, count = forward(bit, held, count)
        started += halo_copies

    for copy in top_copies:
        copy.wait_recv()
    cells = []
    for k in range(slots3):
        name = far3[0, k]
        cell = tops[jnp.maximum(name, 0)]
        cells.append(jnp.where(name >= 0, cell, jnp.zeros_like(cell)))
    top_field = matmul(jnp.concatenate(cells, axis=1), coupling3[...]).astype(jnp.bfloat16)

    @pl.loop(0, clusters)
    def _(b):
        at = lane * clusters + b
        parent = transfer2[at // 8, pl.ds(pl.multiple_of(at % 8 * rank, rank), rank)]
        local = box_far[b] + lax.dot_general(
            top_field, parent, NT, preferred_element_type=jnp.float32
        )
        leaves = lax.dot_general(
            local.astype(jnp.bfloat16), transfer1[b], NT, preferred_element_type=jnp.float32
        ).astype(jnp.bfloat16)
        for u in range(8):
            far_ref[b * 8 + u] = matmul(leaves[:, u * rank : (u + 1) * rank], basis[b * 8 + u])

    for copy in halo_copies:
        copy.wait_recv()
    for copy in started:
        copy.wait_send()


def tree_passes(
    groups,
    subs,
    positions,
    far2_list,
    far3_list,
    bundle,
    inverse,
    basis,
    transfer1,
    coupling2,
    transfer2,
    coupling3,
):
    leaf_dev, rank, points = basis.shape
    clusters = far2_list.shape[0]
    rhs = bundle.shape[1]
    smem = pl.BlockSpec(memory_space=pltpu.SMEM)
    vmem = pl.BlockSpec(memory_space=pltpu.VMEM)
    hbm = pl.BlockSpec(memory_space=pl.ANY)
    dma = pltpu.SemaphoreType.DMA
    return pl.pallas_call(
        functools.partial(tree_kernel, groups, subs),
        out_shape=(
            jax.ShapeDtypeStruct((subs, leaf_dev, rhs, points), jnp.bfloat16),
            jax.ShapeDtypeStruct((2, subs) + bundle.shape, jnp.bfloat16),
            jax.ShapeDtypeStruct((2,) + inverse.shape, jnp.int32),
            jax.ShapeDtypeStruct((leaf_dev, rhs, points), jnp.float32),
        ),
        in_specs=[smem] * 3 + [hbm] * 2 + [vmem] * 5,
        out_specs=(vmem, hbm, hbm, vmem),
        scratch_shapes=[
            pltpu.VMEM((3, subs, clusters, rhs, rank), jnp.bfloat16),
            pltpu.VMEM((groups, rhs, rank), jnp.bfloat16),
            pltpu.VMEM((clusters, rhs, rank), jnp.float32),
            dma((1,)),
            dma((2, subs - 1)),
            dma((2, 2)),
            dma((2, 2)),
            dma((2, 2 * (subs - 1))),
            dma((2, 3 * subs - 1)),
            dma((2, groups - 1)),
        ],
        compiler_params=pltpu.CompilerParams(
            collective_id=0, has_side_effects=True, vmem_limit_bytes=40 * 1024 * 1024
        ),
        name="tree_passes",
    )(
        positions,
        far2_list,
        far3_list,
        bundle,
        inverse,
        basis,
        transfer1.reshape(clusters, -1, rank),
        coupling2.reshape(clusters, -1, rank),
        transfer2.reshape(transfer2.shape[0] // 8, -1, rank),
        coupling3.reshape(-1, rank),
    )


def classes(points):
    return points // 2, 3 * points // 4, points


def near_kernel(
    sizes,
    item_leaf,
    item_start,
    steps,
    near,
    inverse,
    counts,
    target_ref,
    own_features,
    halo_features,
    own_charges,
    halo_charges,
    far_ref,
    out_ref,
    feature_table,
    charge_table,
    target_table,
    squared,
    sems,
):
    leaf_dev, group_size, subs = sizes
    copies = [
        pltpu.make_async_copy(
            own_features, feature_table.at[pl.ds(group_size, group_size)], sems.at[0]
        ),
        pltpu.make_async_copy(
            halo_features.at[0], feature_table.at[pl.ds(0, group_size)], sems.at[1]
        ),
        pltpu.make_async_copy(
            halo_features.at[1], feature_table.at[pl.ds(2 * group_size, group_size)], sems.at[2]
        ),
        pltpu.make_async_copy(
            own_charges, charge_table.at[pl.ds(group_size, group_size)], sems.at[3]
        ),
    ]
    for lane in range(subs):
        for side in range(2):
            copies.append(
                pltpu.make_async_copy(
                    halo_charges.at[side, lane, pl.ds(0, leaf_dev)],
                    charge_table.at[pl.ds(2 * side * group_size + lane * leaf_dev, leaf_dev)],
                    sems.at[4 + 2 * lane + side],
                )
            )
    for copy in copies:
        copy.start()

    @pl.loop(0, leaf_dev // 8)
    def _(block):
        for u in range(8):
            t = block * 8 + u
            turned = target_ref[t].astype(jnp.float32).T
            target_table[t] = turned.astype(jnp.bfloat16)

    out_ref[...] = jnp.zeros_like(out_ref)
    for copy in copies:
        copy.wait()
    dead = 3 * group_size
    feature_table[dead] = feature_table[group_size]
    charge_table[dead] = jnp.zeros(charge_table.shape[1:], charge_table.dtype)

    def distances(step, rows_used):
        for u in range(ITEMS):
            item = step * ITEMS + u
            t = item_leaf[item]
            p = item_start[item]
            rows = [feature_table[near[p + k]] for k in range(SLOTS)]
            squared[u, :rows_used] = jnp.dot(
                target_table[t, :rows_used],
                jnp.concatenate(rows, axis=1),
                preferred_element_type=jnp.float32,
            ).astype(jnp.bfloat16)

    def products(step, rows_used):
        for u in range(ITEMS):
            item = step * ITEMS + u
            t = item_leaf[item]
            p = item_start[item]
            rows = [charge_table[inverse[near[p + k]]] for k in range(SLOTS)]
            out_ref[t, :, :rows_used] += lax.dot_general(
                jnp.concatenate(rows, axis=1),
                lax.rsqrt(squared[u, :rows_used]),
                NT,
                preferred_element_type=jnp.float32,
            )

    for kind, rows_used in enumerate(classes(out_ref.shape[2])):
        distances(steps[kind], rows_used)

        @pl.loop(steps[kind] + 1, steps[kind + 1] + 1)
        def _(step):
            products(step - 1, rows_used)
            distances(step, rows_used)

    place = lax.broadcasted_iota(jnp.int32, out_ref.shape[1:], 1)

    @pl.loop(0, leaf_dev // 8)
    def _(block):
        for u in range(8):
            t = block * 8 + u
            total = out_ref[t] * kernel_scale + far_ref[t]
            out_ref[t] = jnp.where(place < counts[t], total, 0.0)


def near_field(targets, own, halo, own_charges, halo_charges, near, inverse, counts, far, subs):
    leaf_dev, slots = near.shape
    group_size = own.shape[0]
    points = own.shape[2]
    dead = 3 * group_size
    chunks = -(-slots // SLOTS)
    live = jnp.sum((near >= 0).astype(jnp.int32), axis=1)
    used = (live + SLOTS - 1) // SLOTS
    limits = classes(points)
    kind = sum((counts > limit).astype(jnp.int32) for limit in limits[:-1])
    leaf = jnp.arange(leaf_dev, dtype=jnp.int32)
    first = jnp.zeros((leaf_dev,), jnp.int32)
    steps = [jnp.zeros((), jnp.int32)]
    earlier = leaf[None, :] < leaf[:, None]
    for k in range(len(limits)):
        amount = jnp.where(kind == k, used, 0)
        place = steps[-1] * ITEMS + jnp.sum(jnp.where(earlier, amount[None, :], 0), axis=1)
        first = jnp.where(kind == k, place, first)
        steps.append(steps[-1] + (jnp.sum(amount) + ITEMS - 1) // ITEMS)
    steps = jnp.stack(steps)
    capacity = leaf_dev * chunks + (len(limits) + 1) * ITEMS
    item = jnp.arange(capacity, dtype=jnp.int32)[:, None]
    row = chunks * SLOTS
    chosen = (item >= first[None, :]) & (item < (first + used)[None, :])
    item_leaf = jnp.sum(jnp.where(chosen, leaf[None, :], 0), axis=1)
    at = leaf[None, :] * row + SLOTS * (item - first[None, :])
    start = jnp.sum(jnp.where(chosen, at - leaf_dev * row, 0), axis=1) + leaf_dev * row
    padded = jnp.pad(
        jnp.where(near >= 0, near, dead), ((0, 1), (0, row - slots)), constant_values=dead
    ).reshape(-1)
    smem = pl.BlockSpec(memory_space=pltpu.SMEM)
    vmem = pl.BlockSpec(memory_space=pltpu.VMEM)
    hbm = pl.BlockSpec(memory_space=pl.ANY)
    rhs = own_charges.shape[1]
    return pl.pallas_call(
        functools.partial(near_kernel, (leaf_dev, group_size, subs)),
        out_shape=jax.ShapeDtypeStruct((leaf_dev, rhs, points), jnp.float32),
        in_specs=[smem] * 6 + [vmem, hbm, hbm, hbm, hbm, vmem],
        out_specs=vmem,
        scratch_shapes=[
            pltpu.VMEM((dead + 1, FEATURES, points), jnp.bfloat16),
            pltpu.VMEM((dead + 1, rhs, points), jnp.bfloat16),
            pltpu.VMEM((leaf_dev, points, FEATURES), jnp.bfloat16),
            pltpu.VMEM((ITEMS, points, SLOTS * points), jnp.bfloat16),
            pltpu.SemaphoreType.DMA((4 + 2 * subs,)),
        ],
        compiler_params=pltpu.CompilerParams(vmem_limit_bytes=48 * 1024 * 1024),
        name="near_field",
    )(
        item_leaf,
        start,
        steps,
        padded,
        inverse,
        counts,
        targets,
        own,
        halo,
        own_charges,
        halo_charges,
        far,
    )


def on_device(
    coords,
    charges,
    counts,
    morton,
    near_list,
    basis,
    transfer1,
    far2_list,
    coupling2,
    transfer2,
    far3_list,
    coupling3,
):
    lane = lax.axis_index("sub")
    group = lax.axis_index("leaf")
    subs = lax.axis_size("sub")
    leaf_dev, rhs_count, points = charges.shape
    group_size = coords.shape[0]
    start = lane * leaf_dev

    groups = lax.axis_size("leaf")
    number = jnp.arange(group_size, dtype=jnp.int32)
    slot = lax.dynamic_slice_in_dim(morton, start, leaf_dev, 0)
    arriving_counts = jnp.sum(
        jnp.where(slot[:, None] == number[None, :], counts[None, :], 0), axis=1
    )
    place = jnp.arange(points, dtype=jnp.int32)
    masked = jnp.where(
        place[None, None, :] < arriving_counts[:, None, None], charges, jnp.zeros((), charges.dtype)
    )
    planes = coords.transpose(1, 0, 2)
    own_planes = lax.dynamic_slice_in_dim(planes, start, leaf_dev, 1)
    bundle = jnp.concatenate([masked, own_planes.reshape(-1, rhs_count, points)], axis=0)
    inverse = jnp.sum(
        jnp.where(morton[None, :] == number[:, None], number[None, :], 0), axis=1
    )
    own_features = features(planes, False)
    targets = features(own_planes, True)
    arrived, halo, halo_inverse, far_part = tree_passes(
        groups,
        subs,
        lax.dynamic_slice_in_dim(inverse, start, leaf_dev, 0),
        far2_list,
        far3_list,
        bundle,
        inverse.reshape(-1, points),
        basis,
        transfer1,
        coupling2,
        transfer2,
        coupling3,
    )
    arrived = arrived.reshape(group_size, rhs_count, points)
    halo_inverse = halo_inverse.reshape(2, group_size)
    all_inverse = jnp.concatenate(
        [
            halo_inverse[0],
            inverse + group_size,
            halo_inverse[1] + 2 * group_size,
            jnp.full((1,), 3 * group_size, jnp.int32),
        ]
    )
    halo_planes = halo[:, :, leaf_dev:].reshape(2, subs, 3, leaf_dev, points)
    halo_planes = halo_planes.transpose(2, 0, 1, 3, 4).reshape(3, 2 * group_size, points)
    halo_features = features(halo_planes, False).reshape(2, group_size, FEATURES, points)

    base = (group - 1) * group_size
    near = jnp.where(near_list >= 0, near_list - base, -1)
    own_counts = lax.dynamic_slice_in_dim(counts, start, leaf_dev, 0)
    return near_field(
        targets,
        own_features,
        halo_features,
        arrived,
        halo,
        near,
        all_inverse,
        own_counts,
        far_part,
        subs,
    )


def solution(mesh):
    return jax.shard_map(
        on_device,
        mesh=mesh,
        in_specs=(
            P("leaf", None, None),
            P(("leaf", "sub"), None, None),
            P("leaf"),
            P("leaf"),
            P(("leaf", "sub"), None),
            P(("leaf", "sub"), None, None),
            P(("leaf", "sub"), None, None),
            P(("leaf", "sub"), None),
            P(("leaf", "sub"), None, None, None),
            P("leaf", None, None),
            P("leaf", None),
            P("leaf", None, None, None),
        ),
        out_specs=P(("leaf", "sub"), None, None),
        check_vma=False,
    )
```

```python
import functools

import jax
import jax.numpy as jnp
from jax import lax
from jax.experimental import pallas as pl
from jax.experimental.pallas import tpu as pltpu
from jax.sharding import PartitionSpec as P

kernel_scale = 0.07957747154594767
delta_squared = 0.0025
SLOTS = 4
ITEMS = 8
CHUNKS = 4
FEATURES = 16


MESH = pl.DeviceIdType.MESH


def pieces(value):
    high = value.astype(jnp.bfloat16).astype(jnp.float32)
    rest = value - high
    middle = rest.astype(jnp.bfloat16).astype(jnp.float32)
    return high, middle, rest - middle


def placement():
    row = lax.broadcasted_iota(jnp.int32, (8 * FEATURES, 72), 0)
    column = lax.broadcasted_iota(jnp.int32, (8 * FEATURES, 72), 1)
    same = (row // FEATURES == column % 8) & (row % FEATURES == column // 8)
    return jnp.where(same, 1.0, 0.0).astype(jnp.bfloat16)


def features(place, planes, target):
    x, y, z = (plane.astype(jnp.float32) for plane in planes)
    norm = x * x + y * y + z * z
    one = jnp.ones_like(x)
    if target:
        rows = [x, y, z, *pieces(norm + delta_squared), one, one, one]
    else:
        rows = [-2.0 * x, -2.0 * y, -2.0 * z, one, one, one, *pieces(norm)]
    stacked = jnp.concatenate(rows, axis=0).astype(jnp.bfloat16)
    placed = jnp.dot(place, stacked, preferred_element_type=jnp.float32)
    return placed.reshape(8, FEATURES, x.shape[1])


NT = (((1,), (1,)), ((), ()))


def flip(lane, bit):
    return lane + bit - 2 * bit * ((lane // bit) % 2)


def matmul(left, right):
    return jnp.dot(left, right, preferred_element_type=jnp.float32)


def tree_kernel(
    groups,
    subs,
    positions,
    far2,
    far3,
    bundle,
    inverse,
    basis_in,
    transfer1_in,
    coupling2_in,
    transfer2_in,
    coupling3_in,
    own_table,
    halo,
    halo_inverse,
    far_ref,
    basis,
    transfer1,
    coupling2,
    transfer2,
    coupling3,
    boxes,
    tops,
    box_far,
    local_sems,
    own_sems,
    side_sems,
    inverse_sems,
    halo_sems,
    box_sems,
    top_sems,
):
    group = lax.axis_index("leaf")
    lane = lax.axis_index("sub")
    leaf_dev = basis.shape[0]
    clusters = transfer1.shape[0]
    slots2 = far2.shape[1]
    slots3 = far3.shape[1]
    rank = basis.shape[1]
    before = (group + groups - 1) % groups
    after = (group + 1) % groups
    around = [((lane + d) % subs) for d in range(1, subs)]

    barrier = pltpu.get_barrier_semaphore()
    peers = [(group, other) for other in around]
    peers += [(side, other) for side in (before, after) for other in around]
    peers += [((group + d) % groups, lane) for d in range(1, groups)]
    for peer in peers:
        pl.semaphore_signal(barrier, inc=1, device_id=peer, device_id_type=MESH)
    pl.semaphore_wait(barrier, len(peers))

    def run(when, action):
        if when is None:
            action()
        else:

            @pl.when(when)
            def _():
                action()

    def send(source, target, sems, index, device, when=None):
        copy = pltpu.make_async_remote_copy(
            src_ref=source,
            dst_ref=target,
            send_sem=sems.at[0, index],
            recv_sem=sems.at[1, index],
            device_id=device,
            device_id_type=MESH,
        )
        run(when, copy.start)
        return when, copy

    started = []
    weights = [
        pltpu.make_async_copy(source, target, local_sems.at[1 + k])
        for k, (source, target) in enumerate(
            [
                (basis_in, basis),
                (transfer1_in, transfer1),
                (transfer2_in, transfer2),
                (coupling2_in, coupling2),
                (coupling3_in, coupling3),
            ]
        )
    ]
    bits = []
    bit = subs // 2
    while bit:
        bits.append(bit)
        bit //= 2

    charges = bundle.at[pl.ds(0, leaf_dev)]
    keep = [
        pltpu.make_async_copy(charges, own_table.at[lane], local_sems.at[0]),
    ]
    for copy in keep + weights:
        copy.start()
    first = send(charges, own_table.at[lane], own_sems, 0, (group, flip(lane, bits[0])))
    started.append(first)
    inverses = [
        send(inverse, halo_inverse.at[0], inverse_sems, 0, (after, lane)),
        send(inverse, halo_inverse.at[1], inverse_sems, 1, (before, lane)),
    ]
    started += inverses
    part = bundle.shape[0] // CHUNKS
    has_before = group > 0
    has_after = group < groups - 1
    filled = [has_before, has_after]
    arrivals = []
    for chunk in range(CHUNKS):
        span = pl.ds(chunk * part, part)
        pair = [
            send(
                bundle.at[span],
                halo.at[side, lane, span],
                side_sems,
                2 * chunk + side,
                ((after, before)[side], lane),
                (has_after, has_before)[side],
            )
            for side in range(2)
        ]
        started += pair
        arrivals.append(pair)
    for copy in keep:
        copy.wait()
    first[1].wait_recv()
    held = [lane, flip(lane, bits[0])]
    count = 1
    for bit in bits[1:]:
        copies = []
        for block in held:
            copies.append(
                send(
                    own_table.at[block],
                    own_table.at[block],
                    own_sems,
                    count,
                    (group, flip(lane, bit)),
                )
            )
            count += 1
        started += copies
        for _, copy in copies:
            copy.wait_recv()
        held = held + [flip(block, bit) for block in held]

    def forward(bit, held, chunk, stage):
        span = pl.ds(chunk * part, part)
        copies = []
        for k, block in enumerate(held):
            for side in range(2):
                copies.append(
                    send(
                        halo.at[side, block, span],
                        halo.at[side, block, span],
                        halo_sems,
                        2 * (chunk * (subs - 1) + stage + k) + side,
                        (group, flip(lane, bit)),
                        filled[side],
                    )
                )
        return copies

    def received(chunk, copies):
        for side, (_, copy) in zip([0, 1] * len(copies), copies):
            run(filled[side], copy.wait_recv)

    passed = []
    for chunk in range(CHUNKS // 2):
        received(chunk, arrivals[chunk])
        passed.append(forward(bits[0], [lane], chunk, 0))
    for copy in weights[:2]:
        copy.wait()
    mine = boxes.at[1, lane]

    @pl.loop(0, clusters)
    def _(b):
        moments = []
        for u in range(8):
            position = positions[b * 8 + u]
            source = own_table[position // leaf_dev, position % leaf_dev]
            moments.append(
                lax.dot_general(
                    source, basis[b * 8 + u], NT, preferred_element_type=jnp.float32
                ).astype(jnp.bfloat16)
            )
        boxes[1, lane, b] = matmul(jnp.concatenate(moments, axis=1), transfer1[b]).astype(
            jnp.bfloat16
        )

    copies = []
    for other in around:
        copies.append(send(mine, boxes.at[1, lane], box_sems, len(copies), (group, other)))
    for other in [lane] + around:
        copies.append(send(mine, boxes.at[0, lane], box_sems, len(copies), (after, other)))
        copies.append(send(mine, boxes.at[2, lane], box_sems, len(copies), (before, other)))
    started += copies
    box_copies = copies

    for chunk in range(CHUNKS // 2, CHUNKS):
        received(chunk, arrivals[chunk])
        passed.append(forward(bits[0], [lane], chunk, 0))
    for copies in passed:
        started += copies

    for copy in weights[2:]:
        copy.wait()
    for _, copy in box_copies:
        copy.wait_recv()

    def top_step(chunk, total):
        cells = [boxes[1, chunk * 8 // clusters, chunk * 8 % clusters + u] for u in range(8)]
        return total + matmul(jnp.concatenate(cells, axis=1), transfer2[chunk])

    top = lax.fori_loop(
        0, subs * clusters // 8, top_step, jnp.zeros((bundle.shape[1], rank), jnp.float32)
    )
    tops[group] = top.astype(jnp.bfloat16)
    top_copies = [
        send(tops.at[group], tops.at[group], top_sems, d - 1, ((group + d) % groups, lane))
        for d in range(1, groups)
    ]
    started += top_copies

    @pl.loop(0, clusters)
    def _(b):
        cells = []
        for k in range(slots2):
            name = far2[b, k]
            local = jnp.clip(name - (group - 1) * subs * clusters, 0, 3 * subs * clusters - 1)
            side = local // (subs * clusters)
            rest = local % (subs * clusters)
            cell = boxes[side, rest // clusters, rest % clusters]
            cells.append(jnp.where(name >= 0, cell, jnp.zeros_like(cell)))
        box_far[b] = matmul(jnp.concatenate(cells, axis=1), coupling2[b])

    held = [lane, flip(lane, bits[0])]
    stage = 1
    for bit in bits[1:]:
        later = []
        for chunk in range(CHUNKS):
            received(chunk, passed[chunk])
            later.append(forward(bit, held, chunk, stage))
            started += later[-1]
        stage += len(held)
        held = held + [flip(block, bit) for block in held]
        passed = later

    for _, copy in top_copies:
        copy.wait_recv()
    cells = []
    for k in range(slots3):
        name = far3[0, k]
        cell = tops[jnp.maximum(name, 0)]
        cells.append(jnp.where(name >= 0, cell, jnp.zeros_like(cell)))
    top_field = matmul(jnp.concatenate(cells, axis=1), coupling3[...]).astype(jnp.bfloat16)

    @pl.loop(0, clusters)
    def _(b):
        at = lane * clusters + b
        parent = transfer2[at // 8, pl.ds(pl.multiple_of(at % 8 * rank, rank), rank)]
        local = box_far[b] + lax.dot_general(
            top_field, parent, NT, preferred_element_type=jnp.float32
        )
        leaves = lax.dot_general(
            local.astype(jnp.bfloat16), transfer1[b], NT, preferred_element_type=jnp.float32
        ).astype(jnp.bfloat16)
        for u in range(8):
            far_ref[b * 8 + u] = matmul(leaves[:, u * rank : (u + 1) * rank], basis[b * 8 + u])

    for chunk in range(CHUNKS):
        received(chunk, passed[chunk])
    for _, copy in inverses:
        copy.wait_recv()
    for when, copy in started:
        run(when, copy.wait_send)


def tree_passes(
    groups,
    subs,
    positions,
    far2_list,
    far3_list,
    bundle,
    inverse,
    basis,
    transfer1,
    coupling2,
    transfer2,
    coupling3,
):
    leaf_dev, rank, points = basis.shape
    clusters = far2_list.shape[0]
    rhs = bundle.shape[1]
    smem = pl.BlockSpec(memory_space=pltpu.SMEM)
    vmem = pl.BlockSpec(memory_space=pltpu.VMEM)
    hbm = pl.BlockSpec(memory_space=pl.ANY)
    dma = pltpu.SemaphoreType.DMA
    return pl.pallas_call(
        functools.partial(tree_kernel, groups, subs),
        out_shape=(
            jax.ShapeDtypeStruct((subs, leaf_dev, rhs, points), jnp.bfloat16),
            jax.ShapeDtypeStruct((2, subs) + bundle.shape, jnp.bfloat16),
            jax.ShapeDtypeStruct((2,) + inverse.shape, jnp.int32),
            jax.ShapeDtypeStruct((leaf_dev, rhs, points), jnp.float32),
        ),
        in_specs=[smem] * 3 + [hbm] * 7,
        out_specs=(vmem, hbm, hbm, vmem),
        scratch_shapes=[
            pltpu.VMEM(basis.shape, jnp.bfloat16),
            pltpu.VMEM((clusters, 8 * rank, rank), jnp.bfloat16),
            pltpu.VMEM((clusters, far2_list.shape[1] * rank, rank), jnp.bfloat16),
            pltpu.VMEM((transfer2.shape[0] // 8, 8 * rank, rank), jnp.bfloat16),
            pltpu.VMEM((far3_list.shape[1] * rank, rank), jnp.bfloat16),
            pltpu.VMEM((3, subs, clusters, rhs, rank), jnp.bfloat16),
            pltpu.VMEM((groups, rhs, rank), jnp.bfloat16),
            pltpu.VMEM((clusters, rhs, rank), jnp.float32),
            dma((6,)),
            dma((2, subs - 1)),
            dma((2, 2 * CHUNKS)),
            dma((2, 2)),
            dma((2, 2 * CHUNKS * (subs - 1))),
            dma((2, 3 * subs - 1)),
            dma((2, groups - 1)),
        ],
        compiler_params=pltpu.CompilerParams(
            collective_id=0, has_side_effects=True, vmem_limit_bytes=56 * 1024 * 1024
        ),
        name="tree_passes",
    )(
        positions,
        far2_list,
        far3_list,
        bundle,
        inverse,
        basis,
        transfer1.reshape(clusters, -1, rank),
        coupling2.reshape(clusters, -1, rank),
        transfer2.reshape(transfer2.shape[0] // 8, -1, rank),
        coupling3.reshape(-1, rank),
    )


def classes(points):
    return points // 2, 3 * points // 4, points


def near_kernel(
    sizes,
    item_leaf,
    item_start,
    steps,
    near,
    inverse,
    counts,
    target_planes,
    own_planes,
    own_charges,
    halo,
    far_ref,
    out_ref,
    feature_table,
    charge_table,
    target_table,
    halo_planes,
    squared,
    sems,
):
    leaf_dev, group_size, subs = sizes
    blocks = leaf_dev // 8
    plane_copies = [
        pltpu.make_async_copy(
            halo.at[side, lane, pl.ds(leaf_dev, 3 * blocks)],
            halo_planes.at[side, lane],
            sems.at[1, 2 * lane + side],
        )
        for lane in range(subs)
        for side in range(2)
    ]
    copies = [
        pltpu.make_async_copy(
            own_charges, charge_table.at[pl.ds(group_size, group_size)], sems.at[0, 2 * subs]
        )
    ]
    for lane in range(subs):
        for side in range(2):
            copies.append(
                pltpu.make_async_copy(
                    halo.at[side, lane, pl.ds(0, leaf_dev)],
                    charge_table.at[pl.ds(2 * side * group_size + lane * leaf_dev, leaf_dev)],
                    sems.at[0, 2 * lane + side],
                )
            )
    for copy in plane_copies + copies:
        copy.start()
    place = placement()

    @pl.loop(0, blocks // 2)
    def _(pair):
        for v in range(2):
            block = pair * 2 + v
            built = features(place, [target_planes[c * blocks + block] for c in range(3)], True)
            for u in range(8):
                target_table[block * 8 + u] = built[u].T.astype(jnp.bfloat16)

    @pl.loop(0, subs * blocks // 4)
    def _(four):
        for v in range(4):
            block = four * 4 + v
            built = features(
                place, [own_planes[c * subs * blocks + block] for c in range(3)], False
            )
            feature_table[pl.ds(group_size + block * 8, 8)] = built.astype(jnp.bfloat16)

    out_ref[...] = jnp.zeros_like(out_ref)
    for copy in plane_copies:
        copy.wait()

    @pl.loop(0, blocks)
    def _(block):
        for lane in range(subs):
            for side in range(2):
                built = features(
                    place, [halo_planes[side, lane, c * blocks + block] for c in range(3)], False
                )
                begin = 2 * side * group_size + lane * leaf_dev + block * 8
                feature_table[pl.ds(begin, 8)] = built.astype(jnp.bfloat16)

    for copy in copies:
        copy.wait()
    dead = 3 * group_size
    feature_table[dead] = feature_table[group_size]
    charge_table[dead] = jnp.zeros(charge_table.shape[1:], charge_table.dtype)

    def distances(step, rows_used):
        for u in range(ITEMS):
            item = step * ITEMS + u
            t = item_leaf[item]
            p = item_start[item]
            rows = [feature_table[near[p + k]] for k in range(SLOTS)]
            squared[u, :rows_used] = jnp.dot(
                target_table[t, :rows_used],
                jnp.concatenate(rows, axis=1),
                preferred_element_type=jnp.float32,
            ).astype(jnp.bfloat16)

    def products(step, rows_used):
        for u in range(ITEMS):
            item = step * ITEMS + u
            t = item_leaf[item]
            p = item_start[item]
            rows = [charge_table[inverse[near[p + k]]] for k in range(SLOTS)]
            out_ref[t, :, :rows_used] += lax.dot_general(
                jnp.concatenate(rows, axis=1),
                lax.rsqrt(squared[u, :rows_used]),
                NT,
                preferred_element_type=jnp.float32,
            )

    for kind, rows_used in enumerate(classes(out_ref.shape[2])):
        distances(steps[kind], rows_used)

        @pl.loop(steps[kind] + 1, steps[kind + 1] + 1)
        def _(step):
            products(step - 1, rows_used)
            distances(step, rows_used)

    place = lax.broadcasted_iota(jnp.int32, out_ref.shape[1:], 1)

    @pl.loop(0, leaf_dev // 8)
    def _(block):
        for u in range(8):
            t = block * 8 + u
            total = out_ref[t] * kernel_scale + far_ref[t]
            out_ref[t] = jnp.where(place < counts[t], total, 0.0)


def near_field(targets, own, own_charges, halo, near, inverse, counts, far, subs):
    leaf_dev, slots = near.shape
    group_size = own_charges.shape[0]
    points = own.shape[2]
    dead = 3 * group_size
    chunks = -(-slots // SLOTS)
    live = jnp.sum((near >= 0).astype(jnp.int32), axis=1)
    used = (live + SLOTS - 1) // SLOTS
    limits = classes(points)
    kind = sum((counts > limit).astype(jnp.int32) for limit in limits[:-1])
    leaf = jnp.arange(leaf_dev, dtype=jnp.int32)
    first = jnp.zeros((leaf_dev,), jnp.int32)
    steps = [jnp.zeros((), jnp.int32)]
    earlier = leaf[None, :] < leaf[:, None]
    for k in range(len(limits)):
        amount = jnp.where(kind == k, used, 0)
        place = steps[-1] * ITEMS + jnp.sum(jnp.where(earlier, amount[None, :], 0), axis=1)
        first = jnp.where(kind == k, place, first)
        steps.append(steps[-1] + (jnp.sum(amount) + ITEMS - 1) // ITEMS)
    steps = jnp.stack(steps)
    capacity = leaf_dev * chunks + (len(limits) + 1) * ITEMS
    item = jnp.arange(capacity, dtype=jnp.int32)[:, None]
    row = chunks * SLOTS
    chosen = (item >= first[None, :]) & (item < (first + used)[None, :])
    item_leaf = jnp.sum(jnp.where(chosen, leaf[None, :], 0), axis=1)
    at = leaf[None, :] * row + SLOTS * (item - first[None, :])
    start = jnp.sum(jnp.where(chosen, at - leaf_dev * row, 0), axis=1) + leaf_dev * row
    padded = jnp.pad(
        jnp.where(near >= 0, near, dead), ((0, 1), (0, row - slots)), constant_values=dead
    ).reshape(-1)
    smem = pl.BlockSpec(memory_space=pltpu.SMEM)
    vmem = pl.BlockSpec(memory_space=pltpu.VMEM)
    hbm = pl.BlockSpec(memory_space=pl.ANY)
    rhs = own_charges.shape[1]
    return pl.pallas_call(
        functools.partial(near_kernel, (leaf_dev, group_size, subs)),
        out_shape=jax.ShapeDtypeStruct((leaf_dev, rhs, points), jnp.float32),
        in_specs=[smem] * 6 + [vmem, vmem, hbm, hbm, vmem],
        out_specs=vmem,
        scratch_shapes=[
            pltpu.VMEM((dead + 1, FEATURES, points), jnp.bfloat16),
            pltpu.VMEM((dead + 1, rhs, points), jnp.bfloat16),
            pltpu.VMEM((leaf_dev, points, FEATURES), jnp.bfloat16),
            pltpu.VMEM((2, subs, 3 * leaf_dev // 8, 8, points), jnp.bfloat16),
            pltpu.VMEM((ITEMS, points, SLOTS * points), jnp.bfloat16),
            pltpu.SemaphoreType.DMA((2, 2 * subs + 1)),
        ],
        compiler_params=pltpu.CompilerParams(vmem_limit_bytes=48 * 1024 * 1024),
        name="near_field",
    )(
        item_leaf,
        start,
        steps,
        padded,
        inverse,
        counts,
        targets,
        own,
        own_charges,
        halo,
        far,
    )


def on_device(
    coords,
    charges,
    counts,
    morton,
    near_list,
    basis,
    transfer1,
    far2_list,
    coupling2,
    transfer2,
    far3_list,
    coupling3,
):
    lane = lax.axis_index("sub")
    group = lax.axis_index("leaf")
    subs = lax.axis_size("sub")
    leaf_dev, rhs_count, points = charges.shape
    group_size = coords.shape[0]
    start = lane * leaf_dev

    groups = lax.axis_size("leaf")
    number = jnp.arange(group_size, dtype=jnp.int32)
    slot = lax.dynamic_slice_in_dim(morton, start, leaf_dev, 0)
    arriving_counts = jnp.sum(
        jnp.where(slot[:, None] == number[None, :], counts[None, :], 0), axis=1
    )
    place = jnp.arange(points, dtype=jnp.int32)
    masked = jnp.where(
        place[None, None, :] < arriving_counts[:, None, None], charges, jnp.zeros((), charges.dtype)
    )
    planes = coords.transpose(1, 0, 2)
    own_planes = lax.dynamic_slice_in_dim(planes, start, leaf_dev, 1)
    bundle = jnp.concatenate([masked, own_planes.reshape(-1, 8, points)], axis=0)
    inverse = jnp.sum(
        jnp.where(morton[None, :] == number[:, None], number[None, :], 0), axis=1
    )
    arrived, halo, halo_inverse, far_part = tree_passes(
        groups,
        subs,
        lax.dynamic_slice_in_dim(inverse, start, leaf_dev, 0),
        far2_list,
        far3_list,
        bundle,
        inverse.reshape(-1, points),
        basis,
        transfer1,
        coupling2,
        transfer2,
        coupling3,
    )
    arrived = arrived.reshape(group_size, rhs_count, points)
    halo_inverse = halo_inverse.reshape(2, group_size)
    all_inverse = jnp.concatenate(
        [
            halo_inverse[0],
            inverse + group_size,
            halo_inverse[1] + 2 * group_size,
            jnp.full((1,), 3 * group_size, jnp.int32),
        ]
    )
    base = (group - 1) * group_size
    near = jnp.where(near_list >= 0, near_list - base, -1)
    own_counts = lax.dynamic_slice_in_dim(counts, start, leaf_dev, 0)
    return near_field(
        own_planes.reshape(-1, 8, points),
        planes.reshape(-1, 8, points),
        arrived,
        halo,
        near,
        all_inverse,
        own_counts,
        far_part,
        subs,
    )


def solution(mesh):
    return jax.shard_map(
        on_device,
        mesh=mesh,
        in_specs=(
            P("leaf", None, None),
            P(("leaf", "sub"), None, None),
            P("leaf"),
            P("leaf"),
            P(("leaf", "sub"), None),
            P(("leaf", "sub"), None, None),
            P(("leaf", "sub"), None, None),
            P(("leaf", "sub"), None),
            P(("leaf", "sub"), None, None, None),
            P("leaf", None, None),
            P("leaf", None),
            P("leaf", None, None, None),
        ),
        out_specs=P(("leaf", "sub"), None, None),
        check_vma=False,
    )
```

```python
import functools

import jax
import jax.numpy as jnp
from jax import lax
from jax.experimental import pallas as pl
from jax.experimental.pallas import tpu as pltpu
from jax.sharding import PartitionSpec as P

kernel_scale = 0.07957747154594767
delta_squared = 0.0025
SLOTS = 4
ITEMS = 8
CHUNKS = 4
UNROLL = 4
FEATURES = 16


MESH = pl.DeviceIdType.MESH


def pieces(value):
    high = value.astype(jnp.bfloat16).astype(jnp.float32)
    rest = value - high
    middle = rest.astype(jnp.bfloat16).astype(jnp.float32)
    return high, middle, rest - middle


def placement():
    row = lax.broadcasted_iota(jnp.int32, (8 * FEATURES, 72), 0)
    column = lax.broadcasted_iota(jnp.int32, (8 * FEATURES, 72), 1)
    same = (row // FEATURES == column % 8) & (row % FEATURES == column // 8)
    return jnp.where(same, 1.0, 0.0).astype(jnp.bfloat16)


def features(place, planes, target):
    x, y, z = (plane.astype(jnp.float32) for plane in planes)
    norm = x * x + y * y + z * z
    one = jnp.ones_like(x)
    if target:
        rows = [x, y, z, *pieces(norm + delta_squared), one, one, one]
    else:
        rows = [-2.0 * x, -2.0 * y, -2.0 * z, one, one, one, *pieces(norm)]
    stacked = jnp.concatenate(rows, axis=0).astype(jnp.bfloat16)
    placed = jnp.dot(place, stacked, preferred_element_type=jnp.float32)
    return placed.reshape(8, FEATURES, x.shape[1])


NT = (((1,), (1,)), ((), ()))


def flip(lane, bit):
    return lane + bit - 2 * bit * ((lane // bit) % 2)


def matmul(left, right):
    return jnp.dot(left, right, preferred_element_type=jnp.float32)


def tree_kernel(
    groups,
    subs,
    positions,
    far2,
    far3,
    bundle,
    inverse,
    basis_in,
    transfer1_in,
    coupling2_in,
    transfer2_in,
    coupling3_in,
    own_table,
    halo,
    halo_inverse,
    far_ref,
    basis,
    transfer1,
    coupling2,
    transfer2,
    coupling3,
    boxes,
    tops,
    box_far,
    local_sems,
    own_sems,
    side_sems,
    inverse_sems,
    halo_sems,
    box_sems,
    top_sems,
):
    group = lax.axis_index("leaf")
    lane = lax.axis_index("sub")
    leaf_dev = basis.shape[0]
    clusters = transfer1.shape[0]
    slots2 = far2.shape[1]
    slots3 = far3.shape[1]
    rank = basis.shape[1]
    before = (group + groups - 1) % groups
    after = (group + 1) % groups
    around = [((lane + d) % subs) for d in range(1, subs)]

    barrier = pltpu.get_barrier_semaphore()
    peers = [(group, other) for other in around]
    peers += [(side, other) for side in (before, after) for other in around]
    peers += [((group + d) % groups, lane) for d in range(1, groups)]
    for peer in peers:
        pl.semaphore_signal(barrier, inc=1, device_id=peer, device_id_type=MESH)
    pl.semaphore_wait(barrier, len(peers))

    def run(when, action):
        if when is None:
            action()
        else:

            @pl.when(when)
            def _():
                action()

    def send(source, target, sems, index, device, when=None):
        copy = pltpu.make_async_remote_copy(
            src_ref=source,
            dst_ref=target,
            send_sem=sems.at[0, index],
            recv_sem=sems.at[1, index],
            device_id=device,
            device_id_type=MESH,
        )
        run(when, copy.start)
        return when, copy

    started = []
    weights = [
        pltpu.make_async_copy(source, target, local_sems.at[1 + k])
        for k, (source, target) in enumerate(
            [
                (basis_in, basis),
                (transfer1_in, transfer1),
                (transfer2_in, transfer2),
                (coupling2_in, coupling2),
                (coupling3_in, coupling3),
            ]
        )
    ]
    bits = []
    bit = subs // 2
    while bit:
        bits.append(bit)
        bit //= 2

    charges = bundle.at[pl.ds(0, leaf_dev)]
    keep = [
        pltpu.make_async_copy(charges, own_table.at[lane], local_sems.at[0]),
    ]
    for copy in keep + weights:
        copy.start()
    first = send(charges, own_table.at[lane], own_sems, 0, (group, flip(lane, bits[0])))
    started.append(first)
    inverses = [
        send(inverse, halo_inverse.at[0], inverse_sems, 0, (after, lane)),
        send(inverse, halo_inverse.at[1], inverse_sems, 1, (before, lane)),
    ]
    started += inverses
    part = bundle.shape[0] // CHUNKS
    has_before = group > 0
    has_after = group < groups - 1
    filled = [has_before, has_after]
    arrivals = []
    for chunk in range(CHUNKS):
        span = pl.ds(chunk * part, part)
        pair = [
            send(
                bundle.at[span],
                halo.at[side, lane, span],
                side_sems,
                2 * chunk + side,
                ((after, before)[side], lane),
                (has_after, has_before)[side],
            )
            for side in range(2)
        ]
        started += pair
        arrivals.append(pair)
    for copy in keep:
        copy.wait()
    first[1].wait_recv()
    held = [lane, flip(lane, bits[0])]
    count = 1
    for bit in bits[1:]:
        copies = []
        for block in held:
            copies.append(
                send(
                    own_table.at[block],
                    own_table.at[block],
                    own_sems,
                    count,
                    (group, flip(lane, bit)),
                )
            )
            count += 1
        started += copies
        for _, copy in copies:
            copy.wait_recv()
        held = held + [flip(block, bit) for block in held]

    def forward(bit, held, chunk, stage):
        span = pl.ds(chunk * part, part)
        copies = []
        for k, block in enumerate(held):
            for side in range(2):
                copies.append(
                    send(
                        halo.at[side, block, span],
                        halo.at[side, block, span],
                        halo_sems,
                        2 * (chunk * (subs - 1) + stage + k) + side,
                        (group, flip(lane, bit)),
                        filled[side],
                    )
                )
        return copies

    def received(chunk, copies):
        for side, (_, copy) in zip([0, 1] * len(copies), copies):
            run(filled[side], copy.wait_recv)

    passed = []
    for chunk in range(CHUNKS // 2):
        received(chunk, arrivals[chunk])
        passed.append(forward(bits[0], [lane], chunk, 0))
    for copy in weights[:2]:
        copy.wait()
    mine = boxes.at[1, lane]

    def box_moment(b):
        moments = []
        for u in range(8):
            position = positions[b * 8 + u]
            source = own_table[position // leaf_dev, position % leaf_dev]
            moments.append(
                lax.dot_general(
                    source, basis[b * 8 + u], NT, preferred_element_type=jnp.float32
                ).astype(jnp.bfloat16)
            )
        return matmul(jnp.concatenate(moments, axis=1), transfer1[b]).astype(jnp.bfloat16)

    @pl.loop(0, clusters // UNROLL)
    def _(step):
        found = [box_moment(step * UNROLL + v) for v in range(UNROLL)]
        for v in range(UNROLL):
            boxes[1, lane, step * UNROLL + v] = found[v]

    copies = []
    for other in around:
        copies.append(send(mine, boxes.at[1, lane], box_sems, len(copies), (group, other)))
    for other in [lane] + around:
        copies.append(send(mine, boxes.at[0, lane], box_sems, len(copies), (after, other)))
        copies.append(send(mine, boxes.at[2, lane], box_sems, len(copies), (before, other)))
    started += copies
    box_copies = copies

    for chunk in range(CHUNKS // 2, CHUNKS):
        received(chunk, arrivals[chunk])
        passed.append(forward(bits[0], [lane], chunk, 0))
    for copies in passed:
        started += copies

    for copy in weights[2:]:
        copy.wait()
    for _, copy in box_copies:
        copy.wait_recv()

    def top_step(step, total):
        for v in range(UNROLL):
            chunk = step * UNROLL + v
            cells = [boxes[1, chunk * 8 // clusters, chunk * 8 % clusters + u] for u in range(8)]
            total = total + matmul(jnp.concatenate(cells, axis=1), transfer2[chunk])
        return total

    top = lax.fori_loop(
        0, subs * clusters // 8 // UNROLL, top_step, jnp.zeros((bundle.shape[1], rank), jnp.float32)
    )
    tops[group] = top.astype(jnp.bfloat16)
    top_copies = [
        send(tops.at[group], tops.at[group], top_sems, d - 1, ((group + d) % groups, lane))
        for d in range(1, groups)
    ]
    started += top_copies

    def box_field(b):
        cells = []
        for k in range(slots2):
            name = far2[b, k]
            local = jnp.clip(name - (group - 1) * subs * clusters, 0, 3 * subs * clusters - 1)
            side = local // (subs * clusters)
            rest = local % (subs * clusters)
            cell = boxes[side, rest // clusters, rest % clusters]
            cells.append(jnp.where(name >= 0, cell, jnp.zeros_like(cell)))
        return matmul(jnp.concatenate(cells, axis=1), coupling2[b])

    @pl.loop(0, clusters // UNROLL)
    def _(step):
        found = [box_field(step * UNROLL + v) for v in range(UNROLL)]
        for v in range(UNROLL):
            box_far[step * UNROLL + v] = found[v]

    held = [lane, flip(lane, bits[0])]
    stage = 1
    for bit in bits[1:]:
        later = []
        for chunk in range(CHUNKS):
            received(chunk, passed[chunk])
            later.append(forward(bit, held, chunk, stage))
            started += later[-1]
        stage += len(held)
        held = held + [flip(block, bit) for block in held]
        passed = later

    for _, copy in top_copies:
        copy.wait_recv()
    cells = []
    for k in range(slots3):
        name = far3[0, k]
        cell = tops[jnp.maximum(name, 0)]
        cells.append(jnp.where(name >= 0, cell, jnp.zeros_like(cell)))
    top_field = matmul(jnp.concatenate(cells, axis=1), coupling3[...]).astype(jnp.bfloat16)

    def leaf_fields(b):
        at = lane * clusters + b
        parent = transfer2[at // 8, pl.ds(pl.multiple_of(at % 8 * rank, rank), rank)]
        local = box_far[b] + lax.dot_general(
            top_field, parent, NT, preferred_element_type=jnp.float32
        )
        leaves = lax.dot_general(
            local.astype(jnp.bfloat16), transfer1[b], NT, preferred_element_type=jnp.float32
        ).astype(jnp.bfloat16)
        return [
            matmul(leaves[:, u * rank : (u + 1) * rank], basis[b * 8 + u]) for u in range(8)
        ]

    @pl.loop(0, clusters // UNROLL)
    def _(step):
        found = [leaf_fields(step * UNROLL + v) for v in range(UNROLL)]
        for v in range(UNROLL):
            for u in range(8):
                far_ref[(step * UNROLL + v) * 8 + u] = found[v][u]

    for chunk in range(CHUNKS):
        received(chunk, passed[chunk])
    for _, copy in inverses:
        copy.wait_recv()
    for when, copy in started:
        run(when, copy.wait_send)


def tree_passes(
    groups,
    subs,
    positions,
    far2_list,
    far3_list,
    bundle,
    inverse,
    basis,
    transfer1,
    coupling2,
    transfer2,
    coupling3,
):
    leaf_dev, rank, points = basis.shape
    clusters = far2_list.shape[0]
    rhs = bundle.shape[1]
    smem = pl.BlockSpec(memory_space=pltpu.SMEM)
    vmem = pl.BlockSpec(memory_space=pltpu.VMEM)
    hbm = pl.BlockSpec(memory_space=pl.ANY)
    dma = pltpu.SemaphoreType.DMA
    return pl.pallas_call(
        functools.partial(tree_kernel, groups, subs),
        out_shape=(
            jax.ShapeDtypeStruct((subs, leaf_dev, rhs, points), jnp.bfloat16),
            jax.ShapeDtypeStruct((2, subs) + bundle.shape, jnp.bfloat16),
            jax.ShapeDtypeStruct((2,) + inverse.shape, jnp.int32),
            jax.ShapeDtypeStruct((leaf_dev, rhs, points), jnp.float32),
        ),
        in_specs=[smem] * 3 + [hbm] * 7,
        out_specs=(vmem, hbm, hbm, vmem),
        scratch_shapes=[
            pltpu.VMEM(basis.shape, jnp.bfloat16),
            pltpu.VMEM((clusters, 8 * rank, rank), jnp.bfloat16),
            pltpu.VMEM((clusters, far2_list.shape[1] * rank, rank), jnp.bfloat16),
            pltpu.VMEM((transfer2.shape[0] // 8, 8 * rank, rank), jnp.bfloat16),
            pltpu.VMEM((far3_list.shape[1] * rank, rank), jnp.bfloat16),
            pltpu.VMEM((3, subs, clusters, rhs, rank), jnp.bfloat16),
            pltpu.VMEM((groups, rhs, rank), jnp.bfloat16),
            pltpu.VMEM((clusters, rhs, rank), jnp.float32),
            dma((6,)),
            dma((2, subs - 1)),
            dma((2, 2 * CHUNKS)),
            dma((2, 2)),
            dma((2, 2 * CHUNKS * (subs - 1))),
            dma((2, 3 * subs - 1)),
            dma((2, groups - 1)),
        ],
        compiler_params=pltpu.CompilerParams(
            collective_id=0, has_side_effects=True, vmem_limit_bytes=56 * 1024 * 1024
        ),
        name="tree_passes",
    )(
        positions,
        far2_list,
        far3_list,
        bundle,
        inverse,
        basis,
        transfer1.reshape(clusters, -1, rank),
        coupling2.reshape(clusters, -1, rank),
        transfer2.reshape(transfer2.shape[0] // 8, -1, rank),
        coupling3.reshape(-1, rank),
    )


def classes(points):
    return points // 2, 3 * points // 4, points


def near_kernel(
    sizes,
    item_leaf,
    item_start,
    steps,
    near,
    inverse,
    counts,
    target_planes,
    own_planes,
    own_charges,
    halo,
    far_ref,
    out_ref,
    feature_table,
    charge_table,
    target_table,
    halo_planes,
    squared,
    sums,
    sems,
):
    leaf_dev, group_size, subs = sizes
    blocks = leaf_dev // 8
    plane_copies = [
        pltpu.make_async_copy(
            halo.at[side, lane, pl.ds(leaf_dev, 3 * blocks)],
            halo_planes.at[side, lane],
            sems.at[1, 2 * lane + side],
        )
        for lane in range(subs)
        for side in range(2)
    ]
    copies = [
        pltpu.make_async_copy(
            own_charges, charge_table.at[pl.ds(group_size, group_size)], sems.at[0, 2 * subs]
        )
    ]
    for lane in range(subs):
        for side in range(2):
            copies.append(
                pltpu.make_async_copy(
                    halo.at[side, lane, pl.ds(0, leaf_dev)],
                    charge_table.at[pl.ds(2 * side * group_size + lane * leaf_dev, leaf_dev)],
                    sems.at[0, 2 * lane + side],
                )
            )
    for copy in plane_copies + copies:
        copy.start()
    place = placement()

    @pl.loop(0, blocks // 2)
    def _(pair):
        for v in range(2):
            block = pair * 2 + v
            built = features(place, [target_planes[c * blocks + block] for c in range(3)], True)
            for u in range(8):
                target_table[block * 8 + u] = built[u].T.astype(jnp.bfloat16)

    @pl.loop(0, subs * blocks // 4)
    def _(four):
        for v in range(4):
            block = four * 4 + v
            built = features(
                place, [own_planes[c * subs * blocks + block] for c in range(3)], False
            )
            feature_table[pl.ds(group_size + block * 8, 8)] = built.astype(jnp.bfloat16)

    sums[...] = jnp.zeros_like(sums)
    for copy in plane_copies:
        copy.wait()

    @pl.loop(0, blocks)
    def _(block):
        for lane in range(subs):
            for side in range(2):
                built = features(
                    place, [halo_planes[side, lane, c * blocks + block] for c in range(3)], False
                )
                begin = 2 * side * group_size + lane * leaf_dev + block * 8
                feature_table[pl.ds(begin, 8)] = built.astype(jnp.bfloat16)

    for copy in copies:
        copy.wait()
    dead = 3 * group_size
    feature_table[dead] = feature_table[group_size]
    charge_table[dead] = jnp.zeros(charge_table.shape[1:], charge_table.dtype)

    def distances(step, rows_used):
        for u in range(ITEMS):
            item = step * ITEMS + u
            t = item_leaf[item]
            p = item_start[item]
            rows = [feature_table[near[p + k]] for k in range(SLOTS)]
            squared[u, :rows_used] = jnp.dot(
                target_table[t, :rows_used],
                jnp.concatenate(rows, axis=1),
                preferred_element_type=jnp.float32,
            ).astype(jnp.bfloat16)

    def products(step, rows_used):
        for u in range(ITEMS):
            item = step * ITEMS + u
            t = item_leaf[item]
            p = item_start[item]
            rows = [charge_table[inverse[near[p + k]]] for k in range(SLOTS)]
            sums[t, :rows_used] += lax.dot_general(
                lax.rsqrt(squared[u, :rows_used]),
                jnp.concatenate(rows, axis=1),
                NT,
                preferred_element_type=jnp.float32,
            )

    for kind, rows_used in enumerate(classes(out_ref.shape[2])):
        distances(steps[kind], rows_used)

        @pl.loop(steps[kind] + 1, steps[kind + 1] + 1)
        def _(step):
            products(step - 1, rows_used)
            distances(step, rows_used)

    place = lax.broadcasted_iota(jnp.int32, out_ref.shape[1:], 1)

    @pl.loop(0, leaf_dev // 8)
    def _(block):
        for u in range(8):
            t = block * 8 + u
            total = sums[t].T * kernel_scale + far_ref[t]
            out_ref[t] = jnp.where(place < counts[t], total, 0.0)


def near_field(targets, own, own_charges, halo, near, inverse, counts, far, subs):
    leaf_dev, slots = near.shape
    group_size = own_charges.shape[0]
    points = own.shape[2]
    dead = 3 * group_size
    chunks = -(-slots // SLOTS)
    live = jnp.sum((near >= 0).astype(jnp.int32), axis=1)
    used = (live + SLOTS - 1) // SLOTS
    limits = classes(points)
    kind = sum((counts > limit).astype(jnp.int32) for limit in limits[:-1])
    leaf = jnp.arange(leaf_dev, dtype=jnp.int32)
    first = jnp.zeros((leaf_dev,), jnp.int32)
    steps = [jnp.zeros((), jnp.int32)]
    earlier = leaf[None, :] < leaf[:, None]
    for k in range(len(limits)):
        amount = jnp.where(kind == k, used, 0)
        place = steps[-1] * ITEMS + jnp.sum(jnp.where(earlier, amount[None, :], 0), axis=1)
        first = jnp.where(kind == k, place, first)
        steps.append(steps[-1] + (jnp.sum(amount) + ITEMS - 1) // ITEMS)
    steps = jnp.stack(steps)
    capacity = leaf_dev * chunks + (len(limits) + 1) * ITEMS
    item = jnp.arange(capacity, dtype=jnp.int32)[:, None]
    row = chunks * SLOTS
    chosen = (item >= first[None, :]) & (item < (first + used)[None, :])
    item_leaf = jnp.sum(jnp.where(chosen, leaf[None, :], 0), axis=1)
    at = leaf[None, :] * row + SLOTS * (item - first[None, :])
    start = jnp.sum(jnp.where(chosen, at - leaf_dev * row, 0), axis=1) + leaf_dev * row
    padded = jnp.pad(
        jnp.where(near >= 0, near, dead), ((0, 1), (0, row - slots)), constant_values=dead
    ).reshape(-1)
    smem = pl.BlockSpec(memory_space=pltpu.SMEM)
    vmem = pl.BlockSpec(memory_space=pltpu.VMEM)
    hbm = pl.BlockSpec(memory_space=pl.ANY)
    rhs = own_charges.shape[1]
    return pl.pallas_call(
        functools.partial(near_kernel, (leaf_dev, group_size, subs)),
        out_shape=jax.ShapeDtypeStruct((leaf_dev, rhs, points), jnp.float32),
        in_specs=[smem] * 6 + [vmem, vmem, hbm, hbm, vmem],
        out_specs=vmem,
        scratch_shapes=[
            pltpu.VMEM((dead + 1, FEATURES, points), jnp.bfloat16),
            pltpu.VMEM((dead + 1, rhs, points), jnp.bfloat16),
            pltpu.VMEM((leaf_dev, points, FEATURES), jnp.bfloat16),
            pltpu.VMEM((2, subs, 3 * leaf_dev // 8, 8, points), jnp.bfloat16),
            pltpu.VMEM((ITEMS, points, SLOTS * points), jnp.bfloat16),
            pltpu.VMEM((leaf_dev, points, rhs), jnp.float32),
            pltpu.SemaphoreType.DMA((2, 2 * subs + 1)),
        ],
        compiler_params=pltpu.CompilerParams(vmem_limit_bytes=48 * 1024 * 1024),
        name="near_field",
    )(
        item_leaf,
        start,
        steps,
        padded,
        inverse,
        counts,
        targets,
        own,
        own_charges,
        halo,
        far,
    )


def on_device(
    coords,
    charges,
    counts,
    morton,
    near_list,
    basis,
    transfer1,
    far2_list,
    coupling2,
    transfer2,
    far3_list,
    coupling3,
):
    lane = lax.axis_index("sub")
    group = lax.axis_index("leaf")
    subs = lax.axis_size("sub")
    leaf_dev, rhs_count, points = charges.shape
    group_size = coords.shape[0]
    start = lane * leaf_dev

    groups = lax.axis_size("leaf")
    number = jnp.arange(group_size, dtype=jnp.int32)
    slot = lax.dynamic_slice_in_dim(morton, start, leaf_dev, 0)
    arriving_counts = jnp.sum(
        jnp.where(slot[:, None] == number[None, :], counts[None, :], 0), axis=1
    )
    place = jnp.arange(points, dtype=jnp.int32)
    masked = jnp.where(
        place[None, None, :] < arriving_counts[:, None, None], charges, jnp.zeros((), charges.dtype)
    )
    planes = coords.transpose(1, 0, 2)
    own_planes = lax.dynamic_slice_in_dim(planes, start, leaf_dev, 1)
    bundle = jnp.concatenate([masked, own_planes.reshape(-1, 8, points)], axis=0)
    inverse = jnp.sum(
        jnp.where(morton[None, :] == number[:, None], number[None, :], 0), axis=1
    )
    arrived, halo, halo_inverse, far_part = tree_passes(
        groups,
        subs,
        lax.dynamic_slice_in_dim(inverse, start, leaf_dev, 0),
        far2_list,
        far3_list,
        bundle,
        inverse.reshape(-1, points),
        basis,
        transfer1,
        coupling2,
        transfer2,
        coupling3,
    )
    arrived = arrived.reshape(group_size, rhs_count, points)
    halo_inverse = halo_inverse.reshape(2, group_size)
    all_inverse = jnp.concatenate(
        [
            halo_inverse[0],
            inverse + group_size,
            halo_inverse[1] + 2 * group_size,
            jnp.full((1,), 3 * group_size, jnp.int32),
        ]
    )
    base = (group - 1) * group_size
    near = jnp.where(near_list >= 0, near_list - base, -1)
    own_counts = lax.dynamic_slice_in_dim(counts, start, leaf_dev, 0)
    return near_field(
        own_planes.reshape(-1, 8, points),
        planes.reshape(-1, 8, points),
        arrived,
        halo,
        near,
        all_inverse,
        own_counts,
        far_part,
        subs,
    )


def solution(mesh):
    return jax.shard_map(
        on_device,
        mesh=mesh,
        in_specs=(
            P("leaf", None, None),
            P(("leaf", "sub"), None, None),
            P("leaf"),
            P("leaf"),
            P(("leaf", "sub"), None),
            P(("leaf", "sub"), None, None),
            P(("leaf", "sub"), None, None),
            P(("leaf", "sub"), None),
            P(("leaf", "sub"), None, None, None),
            P("leaf", None, None),
            P("leaf", None),
            P("leaf", None, None, None),
        ),
        out_specs=P(("leaf", "sub"), None, None),
        check_vma=False,
    )
```

```python
import functools

import jax
import jax.numpy as jnp
from jax import lax
from jax.experimental import pallas as pl
from jax.experimental.pallas import tpu as pltpu
from jax.sharding import PartitionSpec as P

kernel_scale = 0.07957747154594767
delta_squared = 0.0025
SLOTS = 4
ITEMS = 8
CHUNKS = 4
UNROLL = 4
FEATURES = 16


MESH = pl.DeviceIdType.MESH


def pieces(value):
    high = value.astype(jnp.bfloat16).astype(jnp.float32)
    rest = value - high
    middle = rest.astype(jnp.bfloat16).astype(jnp.float32)
    return high, middle, rest - middle


def placement():
    row = lax.broadcasted_iota(jnp.int32, (8 * FEATURES, 72), 0)
    column = lax.broadcasted_iota(jnp.int32, (8 * FEATURES, 72), 1)
    same = (row // FEATURES == column % 8) & (row % FEATURES == column // 8)
    return jnp.where(same, 1.0, 0.0).astype(jnp.bfloat16)


def features(place, planes, target):
    x, y, z = (plane.astype(jnp.float32) for plane in planes)
    norm = x * x + y * y + z * z
    one = jnp.ones_like(x)
    if target:
        rows = [x, y, z, *pieces(norm + delta_squared), one, one, one]
    else:
        rows = [-2.0 * x, -2.0 * y, -2.0 * z, one, one, one, *pieces(norm)]
    stacked = jnp.concatenate(rows, axis=0).astype(jnp.bfloat16)
    placed = jnp.dot(place, stacked, preferred_element_type=jnp.float32)
    return placed.reshape(8, FEATURES, x.shape[1])


NT = (((1,), (1,)), ((), ()))


def flip(lane, bit):
    return lane + bit - 2 * bit * ((lane // bit) % 2)


def matmul(left, right):
    return jnp.dot(left, right, preferred_element_type=jnp.float32)


def tree_kernel(
    groups,
    subs,
    positions,
    far2,
    far3,
    bundle,
    inverse,
    basis_in,
    transfer1_in,
    coupling2_in,
    transfer2_in,
    coupling3_in,
    own_table,
    halo,
    halo_inverse,
    far_ref,
    basis,
    transfer1,
    coupling2,
    transfer2,
    coupling3,
    boxes,
    tops,
    box_far,
    local_sems,
    own_sems,
    side_sems,
    inverse_sems,
    halo_sems,
    box_sems,
    top_sems,
):
    group = lax.axis_index("leaf")
    lane = lax.axis_index("sub")
    leaf_dev = basis.shape[0]
    clusters = transfer1.shape[0]
    slots2 = far2.shape[1]
    slots3 = far3.shape[1]
    rank = basis.shape[1]
    before = (group + groups - 1) % groups
    after = (group + 1) % groups
    around = [((lane + d) % subs) for d in range(1, subs)]

    barrier = pltpu.get_barrier_semaphore()
    peers = [(group, other) for other in around]
    peers += [(side, other) for side in (before, after) for other in around]
    peers += [((group + d) % groups, lane) for d in range(1, groups)]
    for peer in peers:
        pl.semaphore_signal(barrier, inc=1, device_id=peer, device_id_type=MESH)
    pl.semaphore_wait(barrier, len(peers))

    def run(when, action):
        if when is None:
            action()
        else:

            @pl.when(when)
            def _():
                action()

    def send(source, target, sems, index, device, when=None):
        copy = pltpu.make_async_remote_copy(
            src_ref=source,
            dst_ref=target,
            send_sem=sems.at[0, index],
            recv_sem=sems.at[1, index],
            device_id=device,
            device_id_type=MESH,
        )
        run(when, copy.start)
        return when, copy

    started = []
    weights = [
        pltpu.make_async_copy(source, target, local_sems.at[1 + k])
        for k, (source, target) in enumerate(
            [
                (basis_in, basis),
                (transfer1_in, transfer1),
                (transfer2_in, transfer2),
                (coupling2_in, coupling2),
                (coupling3_in, coupling3),
            ]
        )
    ]
    bits = []
    bit = subs // 2
    while bit:
        bits.append(bit)
        bit //= 2

    charges = bundle.at[pl.ds(0, leaf_dev)]
    keep = [
        pltpu.make_async_copy(charges, own_table.at[lane], local_sems.at[0]),
    ]
    for copy in keep + weights:
        copy.start()
    first = send(charges, own_table.at[lane], own_sems, 0, (group, flip(lane, bits[0])))
    started.append(first)
    inverses = [
        send(inverse, halo_inverse.at[0], inverse_sems, 0, (after, lane)),
        send(inverse, halo_inverse.at[1], inverse_sems, 1, (before, lane)),
    ]
    started += inverses
    part = bundle.shape[0] // CHUNKS
    has_before = group > 0
    has_after = group < groups - 1
    filled = [has_before, has_after]
    arrivals = []
    for chunk in range(CHUNKS):
        span = pl.ds(chunk * part, part)
        pair = [
            send(
                bundle.at[span],
                halo.at[side, lane, span],
                side_sems,
                2 * chunk + side,
                ((after, before)[side], lane),
                (has_after, has_before)[side],
            )
            for side in range(2)
        ]
        started += pair
        arrivals.append(pair)
    for copy in keep:
        copy.wait()
    first[1].wait_recv()
    held = [lane, flip(lane, bits[0])]
    count = 1
    for bit in bits[1:]:
        copies = []
        for block in held:
            copies.append(
                send(
                    own_table.at[block],
                    own_table.at[block],
                    own_sems,
                    count,
                    (group, flip(lane, bit)),
                )
            )
            count += 1
        started += copies
        for _, copy in copies:
            copy.wait_recv()
        held = held + [flip(block, bit) for block in held]

    def forward(bit, held, chunk, stage):
        span = pl.ds(chunk * part, part)
        copies = []
        for k, block in enumerate(held):
            for side in range(2):
                copies.append(
                    send(
                        halo.at[side, block, span],
                        halo.at[side, block, span],
                        halo_sems,
                        2 * (chunk * (subs - 1) + stage + k) + side,
                        (group, flip(lane, bit)),
                        filled[side],
                    )
                )
        return copies

    def received(chunk, copies):
        for side, (_, copy) in zip([0, 1] * len(copies), copies):
            run(filled[side], copy.wait_recv)

    passed = []
    for chunk in range(CHUNKS // 2):
        received(chunk, arrivals[chunk])
        passed.append(forward(bits[0], [lane], chunk, 0))
    for copy in weights[:2]:
        copy.wait()
    mine = boxes.at[1, lane]

    def box_moment(b):
        moments = []
        for u in range(8):
            position = positions[b * 8 + u]
            source = own_table[position // leaf_dev, position % leaf_dev]
            moments.append(
                lax.dot_general(
                    source, basis[b * 8 + u], NT, preferred_element_type=jnp.float32
                ).astype(jnp.bfloat16)
            )
        return matmul(jnp.concatenate(moments, axis=1), transfer1[b]).astype(jnp.bfloat16)

    @pl.loop(0, clusters // UNROLL)
    def _(step):
        found = [box_moment(step * UNROLL + v) for v in range(UNROLL)]
        for v in range(UNROLL):
            boxes[1, lane, step * UNROLL + v] = found[v]

    copies = []
    for other in around:
        copies.append(send(mine, boxes.at[1, lane], box_sems, len(copies), (group, other)))
    for other in [lane] + around:
        copies.append(send(mine, boxes.at[0, lane], box_sems, len(copies), (after, other)))
        copies.append(send(mine, boxes.at[2, lane], box_sems, len(copies), (before, other)))
    started += copies
    box_copies = copies

    for chunk in range(CHUNKS // 2, CHUNKS):
        received(chunk, arrivals[chunk])
        passed.append(forward(bits[0], [lane], chunk, 0))
    for copies in passed:
        started += copies

    for copy in weights[2:]:
        copy.wait()
    for _, copy in box_copies:
        copy.wait_recv()

    def top_step(step, total):
        for v in range(UNROLL):
            chunk = step * UNROLL + v
            cells = [boxes[1, chunk * 8 // clusters, chunk * 8 % clusters + u] for u in range(8)]
            total = total + matmul(jnp.concatenate(cells, axis=1), transfer2[chunk])
        return total

    top = lax.fori_loop(
        0, subs * clusters // 8 // UNROLL, top_step, jnp.zeros((bundle.shape[1], rank), jnp.float32)
    )
    tops[group] = top.astype(jnp.bfloat16)
    top_copies = [
        send(tops.at[group], tops.at[group], top_sems, d - 1, ((group + d) % groups, lane))
        for d in range(1, groups)
    ]
    started += top_copies

    def box_field(b):
        cells = []
        for k in range(slots2):
            name = far2[b, k]
            local = jnp.clip(name - (group - 1) * subs * clusters, 0, 3 * subs * clusters - 1)
            side = local // (subs * clusters)
            rest = local % (subs * clusters)
            cell = boxes[side, rest // clusters, rest % clusters]
            cells.append(jnp.where(name >= 0, cell, jnp.zeros_like(cell)))
        return matmul(jnp.concatenate(cells, axis=1), coupling2[b])

    @pl.loop(0, clusters // UNROLL)
    def _(step):
        found = [box_field(step * UNROLL + v) for v in range(UNROLL)]
        for v in range(UNROLL):
            box_far[step * UNROLL + v] = found[v]

    held = [lane, flip(lane, bits[0])]
    stage = 1
    for bit in bits[1:]:
        later = []
        for chunk in range(CHUNKS):
            received(chunk, passed[chunk])
            later.append(forward(bit, held, chunk, stage))
            started += later[-1]
        stage += len(held)
        held = held + [flip(block, bit) for block in held]
        passed = later

    for _, copy in top_copies:
        copy.wait_recv()
    cells = []
    for k in range(slots3):
        name = far3[0, k]
        cell = tops[jnp.maximum(name, 0)]
        cells.append(jnp.where(name >= 0, cell, jnp.zeros_like(cell)))
    top_field = matmul(jnp.concatenate(cells, axis=1), coupling3[...]).astype(jnp.bfloat16)

    def leaf_fields(b):
        at = lane * clusters + b
        parent = transfer2[at // 8, pl.ds(pl.multiple_of(at % 8 * rank, rank), rank)]
        local = box_far[b] + lax.dot_general(
            top_field, parent, NT, preferred_element_type=jnp.float32
        )
        leaves = lax.dot_general(
            local.astype(jnp.bfloat16), transfer1[b], NT, preferred_element_type=jnp.float32
        ).astype(jnp.bfloat16)
        return [
            matmul(leaves[:, u * rank : (u + 1) * rank], basis[b * 8 + u]) for u in range(8)
        ]

    @pl.loop(0, clusters // UNROLL)
    def _(step):
        found = [leaf_fields(step * UNROLL + v) for v in range(UNROLL)]
        for v in range(UNROLL):
            for u in range(8):
                far_ref[(step * UNROLL + v) * 8 + u] = found[v][u]

    for chunk in range(CHUNKS):
        received(chunk, passed[chunk])
    for _, copy in inverses:
        copy.wait_recv()
    for when, copy in started:
        run(when, copy.wait_send)


def tree_passes(
    groups,
    subs,
    positions,
    far2_list,
    far3_list,
    bundle,
    inverse,
    basis,
    transfer1,
    coupling2,
    transfer2,
    coupling3,
):
    leaf_dev, rank, points = basis.shape
    clusters = far2_list.shape[0]
    rhs = bundle.shape[1]
    smem = pl.BlockSpec(memory_space=pltpu.SMEM)
    vmem = pl.BlockSpec(memory_space=pltpu.VMEM)
    hbm = pl.BlockSpec(memory_space=pl.ANY)
    dma = pltpu.SemaphoreType.DMA
    return pl.pallas_call(
        functools.partial(tree_kernel, groups, subs),
        out_shape=(
            jax.ShapeDtypeStruct((subs, leaf_dev, rhs, points), jnp.bfloat16),
            jax.ShapeDtypeStruct((2, subs) + bundle.shape, jnp.bfloat16),
            jax.ShapeDtypeStruct((2,) + inverse.shape, jnp.int32),
            jax.ShapeDtypeStruct((leaf_dev, rhs, points), jnp.float32),
        ),
        in_specs=[smem] * 3 + [hbm] * 7,
        out_specs=(vmem, hbm, hbm, vmem),
        scratch_shapes=[
            pltpu.VMEM(basis.shape, jnp.bfloat16),
            pltpu.VMEM((clusters, 8 * rank, rank), jnp.bfloat16),
            pltpu.VMEM((clusters, far2_list.shape[1] * rank, rank), jnp.bfloat16),
            pltpu.VMEM((transfer2.shape[0] // 8, 8 * rank, rank), jnp.bfloat16),
            pltpu.VMEM((far3_list.shape[1] * rank, rank), jnp.bfloat16),
            pltpu.VMEM((3, subs, clusters, rhs, rank), jnp.bfloat16),
            pltpu.VMEM((groups, rhs, rank), jnp.bfloat16),
            pltpu.VMEM((clusters, rhs, rank), jnp.float32),
            dma((6,)),
            dma((2, subs - 1)),
            dma((2, 2 * CHUNKS)),
            dma((2, 2)),
            dma((2, 2 * CHUNKS * (subs - 1))),
            dma((2, 3 * subs - 1)),
            dma((2, groups - 1)),
        ],
        compiler_params=pltpu.CompilerParams(
            collective_id=0, has_side_effects=True, vmem_limit_bytes=56 * 1024 * 1024
        ),
        name="tree_passes",
    )(
        positions,
        far2_list,
        far3_list,
        bundle,
        inverse,
        basis,
        transfer1.reshape(clusters, -1, rank),
        coupling2.reshape(clusters, -1, rank),
        transfer2.reshape(transfer2.shape[0] // 8, -1, rank),
        coupling3.reshape(-1, rank),
    )


def classes(points):
    return points // 2, 3 * points // 4, points


def near_kernel(
    sizes,
    item_leaf,
    item_start,
    steps,
    near,
    inverse,
    counts,
    target_planes,
    own_planes,
    own_charges,
    halo,
    far_ref,
    out_ref,
    feature_table,
    charge_table,
    target_table,
    halo_planes,
    squared,
    sems,
):
    leaf_dev, group_size, subs = sizes
    blocks = leaf_dev // 8
    plane_copies = [
        pltpu.make_async_copy(
            halo.at[side, lane, pl.ds(leaf_dev, 3 * blocks)],
            halo_planes.at[side, lane],
            sems.at[1, 2 * lane + side],
        )
        for lane in range(subs)
        for side in range(2)
    ]
    copies = [
        pltpu.make_async_copy(
            own_charges, charge_table.at[pl.ds(group_size, group_size)], sems.at[0, 2 * subs]
        )
    ]
    for lane in range(subs):
        for side in range(2):
            copies.append(
                pltpu.make_async_copy(
                    halo.at[side, lane, pl.ds(0, leaf_dev)],
                    charge_table.at[pl.ds(2 * side * group_size + lane * leaf_dev, leaf_dev)],
                    sems.at[0, 2 * lane + side],
                )
            )
    for copy in plane_copies + copies:
        copy.start()
    place = placement()

    @pl.loop(0, blocks // 2)
    def _(pair):
        for v in range(2):
            block = pair * 2 + v
            built = features(place, [target_planes[c * blocks + block] for c in range(3)], True)
            for u in range(8):
                target_table[block * 8 + u] = built[u].T.astype(jnp.bfloat16)

    @pl.loop(0, subs * blocks // 4)
    def _(four):
        for v in range(4):
            block = four * 4 + v
            built = features(
                place, [own_planes[c * subs * blocks + block] for c in range(3)], False
            )
            feature_table[pl.ds(group_size + block * 8, 8)] = built.astype(jnp.bfloat16)

    out_ref[...] = jnp.zeros_like(out_ref)
    for copy in plane_copies:
        copy.wait()

    @pl.loop(0, blocks)
    def _(block):
        for lane in range(subs):
            for side in range(2):
                built = features(
                    place, [halo_planes[side, lane, c * blocks + block] for c in range(3)], False
                )
                begin = 2 * side * group_size + lane * leaf_dev + block * 8
                feature_table[pl.ds(begin, 8)] = built.astype(jnp.bfloat16)

    for copy in copies:
        copy.wait()
    dead = 3 * group_size
    feature_table[dead] = feature_table[group_size]
    charge_table[dead] = jnp.zeros(charge_table.shape[1:], charge_table.dtype)

    def distances(step, rows_used):
        for u in range(ITEMS):
            item = step * ITEMS + u
            t = item_leaf[item]
            p = item_start[item]
            rows = [feature_table[near[p + k]] for k in range(SLOTS)]
            squared[u, :rows_used] = jnp.dot(
                target_table[t, :rows_used],
                jnp.concatenate(rows, axis=1),
                preferred_element_type=jnp.float32,
            ).astype(jnp.bfloat16)

    def products(step, rows_used):
        for u in range(ITEMS):
            item = step * ITEMS + u
            t = item_leaf[item]
            p = item_start[item]
            rows = [charge_table[inverse[near[p + k]]] for k in range(SLOTS)]
            out_ref[t, :, :rows_used] += lax.dot_general(
                jnp.concatenate(rows, axis=1),
                lax.rsqrt(squared[u, :rows_used]),
                NT,
                preferred_element_type=jnp.float32,
            )

    for kind, rows_used in enumerate(classes(out_ref.shape[2])):
        distances(steps[kind], rows_used)

        @pl.loop(steps[kind] + 1, steps[kind + 1] + 1)
        def _(step):
            products(step - 1, rows_used)
            distances(step, rows_used)

    place = lax.broadcasted_iota(jnp.int32, out_ref.shape[1:], 1)

    @pl.loop(0, leaf_dev // 8)
    def _(block):
        for u in range(8):
            t = block * 8 + u
            total = out_ref[t] * kernel_scale + far_ref[t]
            out_ref[t] = jnp.where(place < counts[t], total, 0.0)


def near_field(targets, own, own_charges, halo, near, inverse, counts, far, subs):
    leaf_dev, slots = near.shape
    group_size = own_charges.shape[0]
    points = own.shape[2]
    dead = 3 * group_size
    chunks = -(-slots // SLOTS)
    live = jnp.sum((near >= 0).astype(jnp.int32), axis=1)
    used = (live + SLOTS - 1) // SLOTS
    limits = classes(points)
    kind = sum((counts > limit).astype(jnp.int32) for limit in limits[:-1])
    leaf = jnp.arange(leaf_dev, dtype=jnp.int32)
    first = jnp.zeros((leaf_dev,), jnp.int32)
    steps = [jnp.zeros((), jnp.int32)]
    earlier = leaf[None, :] < leaf[:, None]
    for k in range(len(limits)):
        amount = jnp.where(kind == k, used, 0)
        place = steps[-1] * ITEMS + jnp.sum(jnp.where(earlier, amount[None, :], 0), axis=1)
        first = jnp.where(kind == k, place, first)
        steps.append(steps[-1] + (jnp.sum(amount) + ITEMS - 1) // ITEMS)
    steps = jnp.stack(steps)
    capacity = leaf_dev * chunks + (len(limits) + 1) * ITEMS
    item = jnp.arange(capacity, dtype=jnp.int32)[:, None]
    row = chunks * SLOTS
    chosen = (item >= first[None, :]) & (item < (first + used)[None, :])
    item_leaf = jnp.sum(jnp.where(chosen, leaf[None, :], 0), axis=1)
    at = leaf[None, :] * row + SLOTS * (item - first[None, :])
    start = jnp.sum(jnp.where(chosen, at - leaf_dev * row, 0), axis=1) + leaf_dev * row
    padded = jnp.pad(
        jnp.where(near >= 0, near, dead), ((0, 1), (0, row - slots)), constant_values=dead
    ).reshape(-1)
    smem = pl.BlockSpec(memory_space=pltpu.SMEM)
    vmem = pl.BlockSpec(memory_space=pltpu.VMEM)
    hbm = pl.BlockSpec(memory_space=pl.ANY)
    rhs = own_charges.shape[1]
    return pl.pallas_call(
        functools.partial(near_kernel, (leaf_dev, group_size, subs)),
        out_shape=jax.ShapeDtypeStruct((leaf_dev, rhs, points), jnp.float32),
        in_specs=[smem] * 6 + [vmem, vmem, hbm, hbm, vmem],
        out_specs=vmem,
        scratch_shapes=[
            pltpu.VMEM((dead + 1, FEATURES, points), jnp.bfloat16),
            pltpu.VMEM((dead + 1, rhs, points), jnp.bfloat16),
            pltpu.VMEM((leaf_dev, points, FEATURES), jnp.bfloat16),
            pltpu.VMEM((2, subs, 3 * leaf_dev // 8, 8, points), jnp.bfloat16),
            pltpu.VMEM((ITEMS, points, SLOTS * points), jnp.bfloat16),
            pltpu.SemaphoreType.DMA((2, 2 * subs + 1)),
        ],
        compiler_params=pltpu.CompilerParams(vmem_limit_bytes=48 * 1024 * 1024),
        name="near_field",
    )(
        item_leaf,
        start,
        steps,
        padded,
        inverse,
        counts,
        targets,
        own,
        own_charges,
        halo,
        far,
    )


def on_device(
    coords,
    charges,
    counts,
    morton,
    near_list,
    basis,
    transfer1,
    far2_list,
    coupling2,
    transfer2,
    far3_list,
    coupling3,
):
    lane = lax.axis_index("sub")
    group = lax.axis_index("leaf")
    subs = lax.axis_size("sub")
    leaf_dev, rhs_count, points = charges.shape
    group_size = coords.shape[0]
    start = lane * leaf_dev

    groups = lax.axis_size("leaf")
    number = jnp.arange(group_size, dtype=jnp.int32)
    slot = lax.dynamic_slice_in_dim(morton, start, leaf_dev, 0)
    arriving_counts = jnp.sum(
        jnp.where(slot[:, None] == number[None, :], counts[None, :], 0), axis=1
    )
    place = jnp.arange(points, dtype=jnp.int32)
    masked = jnp.where(
        place[None, None, :] < arriving_counts[:, None, None], charges, jnp.zeros((), charges.dtype)
    )
    planes = coords.transpose(1, 0, 2)
    own_planes = lax.dynamic_slice_in_dim(planes, start, leaf_dev, 1)
    bundle = jnp.concatenate([masked, own_planes.reshape(-1, 8, points)], axis=0)
    inverse = jnp.sum(
        jnp.where(morton[None, :] == number[:, None], number[None, :], 0), axis=1
    )
    arrived, halo, halo_inverse, far_part = tree_passes(
        groups,
        subs,
        lax.dynamic_slice_in_dim(inverse, start, leaf_dev, 0),
        far2_list,
        far3_list,
        bundle,
        inverse.reshape(-1, points),
        basis,
        transfer1,
        coupling2,
        transfer2,
        coupling3,
    )
    arrived = arrived.reshape(group_size, rhs_count, points)
    halo_inverse = halo_inverse.reshape(2, group_size)
    all_inverse = jnp.concatenate(
        [
            halo_inverse[0],
            inverse + group_size,
            halo_inverse[1] + 2 * group_size,
            jnp.full((1,), 3 * group_size, jnp.int32),
        ]
    )
    base = (group - 1) * group_size
    near = jnp.where(near_list >= 0, near_list - base, -1)
    own_counts = lax.dynamic_slice_in_dim(counts, start, leaf_dev, 0)
    return near_field(
        own_planes.reshape(-1, 8, points),
        planes.reshape(-1, 8, points),
        arrived,
        halo,
        near,
        all_inverse,
        own_counts,
        far_part,
        subs,
    )


def solution(mesh):
    return jax.shard_map(
        on_device,
        mesh=mesh,
        in_specs=(
            P("leaf", None, None),
            P(("leaf", "sub"), None, None),
            P("leaf"),
            P("leaf"),
            P(("leaf", "sub"), None),
            P(("leaf", "sub"), None, None),
            P(("leaf", "sub"), None, None),
            P(("leaf", "sub"), None),
            P(("leaf", "sub"), None, None, None),
            P("leaf", None, None),
            P("leaf", None),
            P("leaf", None, None, None),
        ),
        out_specs=P(("leaf", "sub"), None, None),
        check_vma=False,
    )
```
